512 devices in a mesh: grp: 16 (over z, core), dom: 32 (over y, x).
Axes of the slice: x: 4, y: 8, z: 8, core: 2. Of those that a mesh axis runs over, the one named last changes fastest.
Arguments:
- feats_t: bfloat16 [512, 131072], P('dom', 'grp'), may hold values from -6 to 6
- w_first: bfloat16 [512, 1024], replicated, may hold values from -0.25 to 0.25
- w_second: bfloat16 [1024, 128], replicated, may hold values from -2.5 to 2.5
- stale_rows: bfloat16 [65536, 1152], P(('grp', 'dom')), may hold values from -6 to 6
- tile_vals: bfloat16 [1024, 4, 128, 128], P(('grp', 'dom')), may hold values from 0 to 0.076171875
- tile_src: int32 [1024, 4], P(('grp', 'dom')), may hold values from 0 to 5, as said below
- tile_count: int32 [1024], P(('grp', 'dom')), may hold values from 1 to 4, as said below
- labels: int32 [131072], P(('grp', 'dom')), may hold values from 0 to 127
Outputs:
- logits: bfloat16 [131072, 128], P(('grp', 'dom'))
- grad_feats: bfloat16 [512, 131072], P('dom', 'grp')
- grad_first: float32 [512, 1024], P('dom')
- grad_second: float32 [1024, 128], P('dom')
The draws below stay inside these ranges and needn't reach their ends.
Inputs may be any that keep to these rules, and one draw needn't show every extreme that they name: `tile_src`: the 4 entries of one block row are distinct. Slots from tile_count on are not used; in every partition some block row holds that partition's largest count, and some partition reaches 4.
All inputs are finite; a program needn't handle non-finite values.
Results may differ from the reference program's by a relative error of at most 0.025.
Values may be sent and summed in bfloat16 or wider, within the bound.
No kernel may reach another device: no remote copies, remote signals or barrier semaphores. Data moves between devices by JAX's collectives and lax.ppermute only.
A program may use at most 64 MiB of HBM per device.

```python
import jax
import jax.numpy as jnp
from jax import lax

F = 512
HID = 1024
CLS = 128
V_DEV = 256
BLK = 128
SLOTS = 4
EDGE_BLOCKS = 1
VERTS = 131072
N_GRP = 16
N_DOM = 32


def draw_tile_src(key, part):
    key = jax.random.fold_in(key, 11)
    window_blocks = V_DEV // BLK + 2 + 2 * EDGE_BLOCKS
    block_total = VERTS // BLK
    key_list = jax.random.split(key, block_total)

    def choose(single):
        return jax.random.permutation(single, window_blocks)[:SLOTS]
    return jax.vmap(choose)(key_list).astype(jnp.int32)


def draw_tile_count(key, part):
    key = jax.random.fold_in(key, 23)
    partitions = VERTS // V_DEV
    block_count = V_DEV // BLK
    level_key, force_key, count_key, place_key = jax.random.split(key, 4)
    levels = jax.random.randint(level_key, (partitions,), 1, SLOTS + 1)
    chosen = jax.random.randint(force_key, (), 0, partitions)
    levels = levels.at[chosen].set(SLOTS)
    counts = jax.random.randint(count_key, (partitions, block_count), 1, levels[:, None] + 1)
    peak_at = jax.random.randint(place_key, (partitions,), 0, block_count)
    marker = jnp.arange(block_count)[None, :] == peak_at[:, None]
    counts = jnp.where(marker, levels[:, None], counts)
    return counts.reshape(-1).astype(jnp.int32)


def set_ends(values, key, smallest, largest):
    extent = values.shape
    spot = [jax.random.randint(jax.random.fold_in(key, axis), (), 0, extent[axis]) for axis in range(len(extent))]
    values = values.at[tuple(spot)].set(smallest)
    longest = extent.index(max(extent))
    spot[longest] = (spot[longest] + 1) % extent[longest]
    return values.at[tuple(spot)].set(largest)


def with_spikes(values, key, source, target, shards_of, factor):
    def block_of(dim):
        return (jnp.arange(values.shape[dim]) // (values.shape[dim] // shards_of)).reshape((-1,) + (1,) * (values.ndim - 1 - dim))

    first = jax.random.permutation(key, shards_of)[block_of(target)]
    second = (block_of(target) + shards_of // 2) % shards_of
    return jnp.where((block_of(source) == first) | (block_of(source) == second), factor * values, values)


def shard_levels(own_key, shape, cuts, low, high):
    def one(axis_at, parts):
        heights = jax.random.uniform(jax.random.fold_in(jax.random.fold_in(own_key, 6), axis_at), (parts,), jnp.float32, low / len(cuts), high / len(cuts))
        return jnp.repeat(jnp.exp(heights), shape[axis_at] // parts).reshape((-1,) + (1,) * (len(shape) - axis_at - 1))

    level = one(*cuts[0])
    for cut in cuts[1:]:
        level = level * one(*cut)
    return level


def gaussian(key, extent, scale, bound, cuts=(), kind=jnp.bfloat16):
    gain = shard_levels(key, extent, cuts, -0.22, 0.18) if cuts else 1.0
    values = jax.random.normal(key, extent, jnp.float32) * scale * gain
    return jnp.minimum(jnp.maximum(values, -bound), bound).astype(kind)


def noise_with(key, dims, scale, limit, pieces, heavy, kind=jnp.bfloat16):
    array = scale * jax.random.normal(key, dims, jnp.float32)
    if pieces:
        array = array * shard_levels(key, dims, pieces, -0.22, 0.18)
    return jnp.clip(with_spikes(array, jax.random.fold_in(key, 3), *heavy), -limit, limit).astype(kind)


def setup_inputs(seed: int = 0) -> dict:
    key_of = jax.random.split(jax.random.key(seed), 9)
    return {
        "feats_t": noise_with(key_of[0], (F, VERTS), 1.0, 6.0, ((0, 32), (1, 16)), (1, 0, 32, 2.75)),
        "w_first": gaussian(key_of[1], (F, HID), F ** -0.5, 0.25),
        "w_second": gaussian(key_of[2], (HID, CLS), (5.0 * HID ** -0.5), 2.5),
        "stale_rows": gaussian(key_of[3], (VERTS // V_DEV * EDGE_BLOCKS * BLK, HID + CLS), 1.0, 6.0, ((0, 512),)),
        "tile_vals": jnp.clip(0.076171875 * jax.random.uniform(key_of[4], (VERTS // BLK, SLOTS, BLK, BLK), jnp.float32) ** shard_levels(key_of[4], (VERTS // BLK, SLOTS, BLK, BLK), ((0, 512),), -0.2, 0.2), 0.0, 0.076171875).astype(jnp.bfloat16),
        "tile_src": draw_tile_src(jax.random.fold_in(key_of[8], 71), 0),
        "tile_count": draw_tile_count(jax.random.fold_in(key_of[8], 71), 0),
        "labels": set_ends(jax.random.randint(key_of[7], (VERTS,), 0, CLS), jax.random.fold_in(key_of[7], 1), 0, CLS - 1).astype(jnp.int32),
    }


def build_window(values, stale_before, stale_after, block_rows):
    partitions, own_count, columns = values.shape
    zero = jnp.zeros((1, block_rows, columns), values.dtype)
    left_rim = jnp.concatenate([zero, values[:-1, own_count - block_rows:]], axis=0)
    right_rim = jnp.concatenate([values[1:, :block_rows], zero], axis=0)
    whole = jnp.concatenate([left_rim, values, right_rim, stale_before, stale_after], axis=1)
    return whole.reshape(partitions, whole.shape[1] // block_rows, block_rows, columns)

def live_tiles(tiles, counts):
    slot_total = tiles.shape[2]
    live_mask = jnp.arange(slot_total, dtype=jnp.int32)[None, None, :] < counts[:, :, None]
    return tiles.astype(jnp.float32) * live_mask[:, :, :, None, None].astype(jnp.float32)

def aggregate(window, tiles_live, sources):
    picked = jax.vmap(lambda blocks, chosen: blocks[chosen])(window, sources).astype(jnp.float32)
    result = jnp.einsum('prkab,prkbw->praw', tiles_live, picked)
    return result.reshape(result.shape[0], -1, result.shape[-1])

def spread(grads, tiles_live, sources, block_rows):
    partitions, own_count, columns = grads.shape
    block_count = own_count // block_rows
    blocks = grads.astype(jnp.float32).reshape(partitions, block_count, block_rows, columns)
    terms = jnp.einsum('prkab,praw->prkbw', tiles_live, blocks)
    reach_count = block_count + 2

    def place(chosen, contrib):
        inside = chosen < reach_count
        target = jnp.where(inside, chosen, 0)
        contrib = contrib * inside[:, :, None, None].astype(contrib.dtype)
        return jnp.zeros((reach_count, block_rows, columns), contrib.dtype).at[target].add(contrib)
    placed = jax.vmap(place)(sources, terms)
    own_rows = placed[:, 1:-1].reshape(partitions, own_count, columns)
    zero = jnp.zeros((1, block_rows, columns), own_rows.dtype)
    to_last = jnp.concatenate([placed[1:, 0], zero], axis=0)
    to_first = jnp.concatenate([zero, placed[:-1, -1]], axis=0)
    own_rows = own_rows.at[:, own_count - block_rows:].add(to_last)
    own_rows = own_rows.at[:, :block_rows].add(to_first)
    return own_rows

def reference(feats_t, w_first, w_second, stale_rows, tile_vals, tile_src, tile_count, labels):
    block_rows = BLK
    hidden_width = HID
    block_count = V_DEV // BLK
    feats_groups = feats_t.reshape(F, N_GRP, N_DOM * V_DEV).transpose(1, 0, 2)
    stale = stale_rows.reshape(N_GRP, N_DOM, EDGE_BLOCKS * BLK, HID + CLS)
    zero_band = jnp.zeros((1,) + stale.shape[1:], stale.dtype)
    stale_prev = jnp.concatenate([zero_band, stale[:-1]], axis=0)
    stale_next = jnp.concatenate([stale[1:], zero_band], axis=0)
    tiles = tile_vals.reshape(N_GRP, N_DOM, block_count, SLOTS, BLK, BLK)
    sources = tile_src.reshape(N_GRP, N_DOM, block_count, SLOTS)
    counts = tile_count.reshape(N_GRP, N_DOM, block_count)
    marks = labels.reshape(N_GRP, N_DOM, V_DEV)

    def one_band(inputs):
        feats, before, after, band_tiles, band_sources, band_counts, band_marks = inputs
        tiles_live = live_tiles(band_tiles, band_counts)
        proj_first = jnp.dot(feats.T, w_first, preferred_element_type=jnp.float32).astype(jnp.bfloat16)
        proj_first = proj_first.reshape(N_DOM, V_DEV, hidden_width)
        window_first = build_window(proj_first, before[:, :, :hidden_width], after[:, :, :hidden_width], block_rows)
        agg_first = aggregate(window_first, tiles_live, band_sources)
        squash = jax.nn.sigmoid(agg_first)
        hidden = (agg_first * squash).astype(jnp.bfloat16)
        hidden_flat = hidden.reshape(-1, hidden_width)
        proj_second = jnp.dot(hidden_flat, w_second, preferred_element_type=jnp.float32).astype(jnp.bfloat16)
        proj_second = proj_second.reshape(N_DOM, V_DEV, CLS)
        window_second = build_window(proj_second, before[:, :, hidden_width:], after[:, :, hidden_width:], block_rows)
        agg_second = aggregate(window_second, tiles_live, band_sources)
        logits = agg_second.astype(jnp.bfloat16)
        top_value = lax.optimization_barrier(jnp.max(agg_second, axis=-1, keepdims=True))
        exp_logits = jnp.exp(agg_second - top_value)
        predicted = exp_logits / lax.optimization_barrier(jnp.sum(exp_logits, axis=-1, keepdims=True))
        label_mask = (band_marks[:, :, None] == jnp.arange(CLS, dtype=jnp.int32)[None, None, :]).astype(jnp.float32)
        grad_logits = (predicted - label_mask).astype(jnp.bfloat16)
        grad_p2 = spread(grad_logits, tiles_live, band_sources, block_rows).astype(jnp.bfloat16)
        grad_p2_flat = grad_p2.reshape(-1, CLS)
        second_term = jnp.dot(hidden_flat.T, grad_p2_flat, preferred_element_type=jnp.float32)
        grad_hidden = jnp.dot(grad_p2_flat, w_second.T, preferred_element_type=jnp.float32)
        grad_hidden = grad_hidden.reshape(N_DOM, V_DEV, hidden_width)
        grad_agg = (grad_hidden * squash * (1.0 + agg_first * (1.0 - squash))).astype(jnp.bfloat16)
        grad_p1 = spread(grad_agg, tiles_live, band_sources, block_rows).astype(jnp.bfloat16)
        grad_p1_flat = grad_p1.reshape(-1, hidden_width)
        first_term = jnp.dot(feats, grad_p1_flat, preferred_element_type=jnp.float32)
        grad_band = jnp.dot(w_first, grad_p1_flat.T, preferred_element_type=jnp.float32).astype(jnp.bfloat16)
        return (logits.reshape(-1, CLS), grad_band, first_term, second_term)
    logits, grad_bands, first_terms, second_terms = lax.map(one_band, (feats_groups, stale_prev, stale_next, tiles, sources, counts, marks))
    norm_factor = jnp.sqrt(jnp.float32(VERTS))
    grad_first = lax.optimization_barrier(jnp.sum(first_terms, axis=0)) / norm_factor
    grad_second = lax.optimization_barrier(jnp.sum(second_terms, axis=0)) / norm_factor
    grad_feats = grad_bands.transpose(1, 0, 2).reshape(F, VERTS)
    return (logits.reshape(VERTS, CLS), grad_feats, grad_first, grad_second)
```

```python
import math

import jax
import jax.numpy as jnp
from jax import lax
from jax.sharding import PartitionSpec as P

BF = jnp.bfloat16
F32 = jnp.float32


def dot(a, b, ca, cb):
    return lax.dot_general(a, b, (((ca,), (cb,)), ((), ())), preferred_element_type=F32)


def swapped(x, axis):
    count = lax.axis_size(axis)
    return lax.ppermute(x, axis, [(i, i ^ 1) for i in range(count)])


def from_previous(x, axis):
    count = lax.axis_size(axis)
    return lax.ppermute(x, axis, [(i, i + 1) for i in range(count - 1)])


def from_next(x, axis):
    count = lax.axis_size(axis)
    return lax.ppermute(x, axis, [(i + 1, i) for i in range(count - 1)])


def adjacency(tile_vals, tile_src, tile_count, window_blocks):
    block_rows, slots, blk, _ = tile_vals.shape
    live = jnp.arange(slots, dtype=jnp.int32)[None, :] < tile_count[:, None]
    columns = []
    for t in range(window_blocks):
        hit = (tile_src == t) & live
        block = jnp.zeros((block_rows, blk, blk), BF)
        for k in range(slots):
            block = jnp.where(hit[:, k, None, None], tile_vals[:, k], block)
        columns.append(block.reshape(block_rows * blk, blk))
    return jnp.concatenate(columns, axis=1)


def local(feats_t, w_first, w_second, stale_rows, tile_vals, tile_src, tile_count, labels):
    blk = tile_vals.shape[-1]
    hid = w_first.shape[1]
    classes = w_second.shape[1]
    own = labels.shape[0]
    reach = own + 2 * blk
    n_grp, n_dom = lax.axis_size("grp"), lax.axis_size("dom")
    scale = 1.0 / math.sqrt(own * n_grp * n_dom)
    feat_rows = feats_t.shape[0]
    feat_all = feat_rows * n_dom
    half = hid // 2
    core = lax.axis_index("grp") % 2

    parts = feats_t.reshape(feat_rows, n_dom, own)
    edge = jnp.zeros((feat_rows, 1, blk), BF)
    left = jnp.concatenate([edge, parts[:, :-1, own - blk :]], axis=1)
    right = jnp.concatenate([parts[:, 1:, :blk], edge], axis=1)
    wide = jnp.concatenate([left, parts, right], axis=2)
    feats = lax.all_to_all(wide, "dom", split_axis=1, concat_axis=0, tiled=True).reshape(feat_all, reach)

    before = from_previous(stale_rows, "grp")
    after = from_next(stale_rows, "grp")
    adj_all = adjacency(tile_vals, tile_src, tile_count, reach // blk + 2)
    adj = adj_all[:, :reach]
    stale_part = dot(adj_all[:, reach:], jnp.concatenate([before, after], axis=0), 1, 0)

    feats_agg = dot(adj, feats, 1, 1).astype(BF)
    agg_first = dot(feats_agg, w_first, 1, 0) + stale_part[:, :hid]
    squash = jax.nn.sigmoid(agg_first)
    hidden = (agg_first * squash).astype(BF)
    proj_second = dot(hidden, w_second, 1, 0).astype(BF)

    window = jnp.concatenate(
        [from_previous(proj_second[own - blk :], "dom"), proj_second, from_next(proj_second[:blk], "dom")], axis=0
    )
    agg_second = dot(adj, window, 1, 0) + stale_part[:, hid:]
    logits = agg_second.astype(BF)
    top_value = jnp.max(agg_second, axis=1, keepdims=True)
    exp_logits = jnp.exp(agg_second - top_value)
    predicted = exp_logits / jnp.sum(exp_logits, axis=1, keepdims=True)
    mark = (labels[:, None] == jnp.arange(classes, dtype=jnp.int32)[None, :]).astype(F32)
    grad_logits = (predicted - mark).astype(BF)

    spread_second = dot(adj, grad_logits, 0, 0)
    to_first = from_previous(spread_second[reach - blk :].astype(BF), "dom").astype(F32)
    to_last = from_next(spread_second[:blk].astype(BF), "dom").astype(F32)
    inner = jnp.zeros((own - blk, classes), F32)
    grad_p2 = (
        spread_second[blk : reach - blk]
        + jnp.concatenate([to_first, inner], axis=0)
        + jnp.concatenate([inner, to_last], axis=0)
    ).astype(BF)

    grad_hidden = dot(grad_p2, w_second, 1, 1)
    grad_agg = (grad_hidden * squash * (1.0 + agg_first * (1.0 - squash))).astype(BF)
    first_term = (dot(feats_agg, grad_agg, 0, 0) * scale).astype(BF)
    second_term = (dot(hidden, grad_p2, 0, 0) * scale).astype(BF)
    first_pair = jnp.stack([first_term[:, :half], first_term[:, half:]])
    second_pair = second_term.reshape(n_dom, 2, feat_rows, classes).transpose(1, 0, 2, 3).reshape(2, feat_all, classes)
    both = jnp.concatenate([first_pair, second_pair], axis=2)
    keep = lax.dynamic_index_in_dim(both, core, 0, keepdims=False)
    send = lax.dynamic_index_in_dim(both, 1 - core, 0, keepdims=False)
    summed = (keep.astype(F32) + swapped(send, "grp").astype(F32)).astype(BF)

    back = dot(grad_agg, w_first, 1, 1).astype(BF)
    grad_wide = dot(back, adj, 0, 0).astype(BF)
    sent = jnp.concatenate([summed, grad_wide], axis=1)
    got = lax.all_to_all(sent, "dom", split_axis=0, concat_axis=0, tiled=True).reshape(n_dom, feat_rows, -1)

    width = half + classes
    band = jnp.sum(got[:, :, :width].astype(F32), axis=0).astype(BF)
    copies = jnp.broadcast_to(band[None], (n_grp, feat_rows, width))
    bands = lax.all_to_all(copies, "grp", split_axis=0, concat_axis=0, tiled=True)
    total = jnp.sum(bands.reshape(n_grp // 2, 2, feat_rows, width).astype(F32), axis=0)
    grad_first = jnp.concatenate([total[0, :, :half], total[1, :, :half]], axis=1)
    grad_second = total[:, :, half:].reshape(2 * feat_rows, classes)

    wide_back = got[:, :, width:].astype(F32)
    none = jnp.zeros((1, feat_rows, blk), F32)
    first_block = jnp.concatenate([none, wide_back[:-1, :, reach - blk :]], axis=0)
    last_block = jnp.concatenate([wide_back[1:, :, :blk], none], axis=0)
    middle = jnp.zeros((n_dom, feat_rows, own - blk), F32)
    grad_feats = (
        wide_back[:, :, blk : reach - blk]
        + jnp.concatenate([first_block, middle], axis=2)
        + jnp.concatenate([middle, last_block], axis=2)
    )
    grad_feats = grad_feats.astype(BF).transpose(1, 0, 2).reshape(feat_rows, n_dom * own)
    return (logits, grad_feats, grad_first, grad_second)


def solution(mesh):
    return jax.shard_map(
        local,
        mesh=mesh,
        in_specs=(
            P("dom", "grp"),
            P(),
            P(),
            P(("grp", "dom"), None),
            P(("grp", "dom"), None, None, None),
            P(("grp", "dom"), None),
            P(("grp", "dom")),
            P(("grp", "dom")),
        ),
        out_specs=(P(("grp", "dom"), None), P("dom", "grp"), P("dom", None), P("dom", None)),
        check_vma=False,
    )
```

```python
import functools
import math

import jax
import jax.numpy as jnp
from jax import lax
from jax.experimental import pallas as pl
from jax.experimental.pallas import tpu as pltpu
from jax.sharding import PartitionSpec as P

BF = jnp.bfloat16
F32 = jnp.float32


def dot(a, b, ca, cb):
    return lax.dot_general(a, b, (((ca,), (cb,)), ((), ())), preferred_element_type=F32)


def swapped(x, axis):
    count = lax.axis_size(axis)
    return lax.ppermute(x, axis, [(i, i ^ 1) for i in range(count)])


def from_previous(x, axis):
    count = lax.axis_size(axis)
    return lax.ppermute(x, axis, [(i, i + 1) for i in range(count - 1)])


def from_next(x, axis):
    count = lax.axis_size(axis)
    return lax.ppermute(x, axis, [(i + 1, i) for i in range(count - 1)])


def adjacency(tile_vals, tile_src, tile_count, window_blocks):
    block_rows, slots, blk, _ = tile_vals.shape
    live = jnp.arange(slots, dtype=jnp.int32)[None, :] < tile_count[:, None]
    columns = []
    for t in range(window_blocks):
        hit = (tile_src == t) & live
        block = jnp.zeros((block_rows, blk, blk), BF)
        for k in range(slots):
            block = jnp.where(hit[:, k, None, None], tile_vals[:, k], block)
        columns.append(block.reshape(block_rows * blk, blk))
    return jnp.concatenate(columns, axis=1)


def whole(kernel, outs, scratch=(), flops=0):
    return pl.pallas_call(
        kernel,
        out_shape=[jax.ShapeDtypeStruct(shape, dtype) for shape, dtype in outs],
        scratch_shapes=list(scratch),
        compiler_params=pltpu.CompilerParams(vmem_limit_bytes=40 * 1024 * 1024),
        cost_estimate=pl.CostEstimate(flops=flops, bytes_accessed=4_000_000, transcendentals=0),
    )


def forward_kernel(adj, feats, w_first, stale, w_second, agg_t, hidden, slope, proj):
    width = feats.shape[1]
    hid = w_first.shape[1]
    step = min(256, hid)
    m = adj[:, :width]
    agg = dot(m, feats[...], 1, 1).astype(BF)
    agg_t[...] = dot(feats[...], m, 1, 1).astype(BF)
    total = jnp.zeros(proj.shape, F32)
    for at in range(0, hid, step):
        cols = slice(at, at + step)
        a = dot(agg, w_first[:, cols], 1, 0) + stale[:, cols]
        s = jax.nn.sigmoid(a)
        h = (a * s).astype(BF)
        hidden[:, cols] = h
        slope[:, cols] = s * (1.0 + a * (1.0 - s))
        total += dot(h, w_second[cols, :], 1, 0)
    proj[...] = total.astype(BF)


def middle_kernel(hid, adj, up, own, down, stale, mark, logits, inner, rim_up, rim_down):
    blk = up.shape[0]
    size = own.shape[0]
    reach = size + 2 * blk
    agg = dot(adj[:, :blk], up[...], 1, 0)
    agg += dot(adj[:, blk : blk + size], own[...], 1, 0)
    agg += dot(adj[:, blk + size : reach], down[...], 1, 0)
    agg += stale[:, hid:]
    logits[...] = agg.astype(BF)
    e = jnp.exp(agg - jnp.max(agg, axis=1, keepdims=True))
    grad = (e / jnp.sum(e, axis=1, keepdims=True) - mark[...]).astype(BF)
    spread = dot(adj[:, :reach], grad, 0, 0)
    inner[...] = spread[blk : blk + size]
    rim_up[...] = spread[:blk].astype(BF)
    rim_down[...] = spread[blk + size :].astype(BF)


def backward_kernel(scale, core, inner, up, down, hidden, w_second, slope, agg_t, send, keep, grad_agg, second):
    blk = up.shape[0]
    size = inner.shape[0]
    hid = slope.shape[1]
    step = min(256, hid)
    half = hid // 2
    other = 1 - core[0]
    upper = inner[:blk] + up[...].astype(F32)
    lower = inner[size - blk :] + down[...].astype(F32)
    if size > 2 * blk:
        parts = [upper, inner[blk : size - blk], lower]
    else:
        parts = [upper, lower]
    grad_p2 = jnp.concatenate(parts, axis=0).astype(BF)
    for at in range(0, hid, step):
        cols = slice(at, at + step)
        grad_agg[:, cols] = (dot(grad_p2, w_second[cols, :], 1, 1) * slope[:, cols]).astype(BF)
    second[...] = (dot(hidden[...], grad_p2, 0, 0) * scale).reshape(second.shape)
    rows = second.shape[0] * second.shape[2]
    send[:, half:] = second[:, other].reshape(rows, second.shape[3]).astype(BF)
    keep[:, half:] = second[:, core[0]].reshape(rows, second.shape[3])
    for mine, out in ((other, send), (core[0], keep)):
        g = grad_agg[:, pl.ds(pl.multiple_of(mine * half, half), half)]
        out[:, :half] = (dot(agg_t[...], g, 1, 0) * scale).astype(out.dtype)


def feature_kernel(grad_agg, w_first, adj, out):
    width = out.shape[1]
    back = dot(w_first[...], grad_agg[...], 1, 1).astype(BF)
    out[...] = dot(back, adj[:, :width], 1, 0).astype(BF)


def whole_core(kernel, outs, blocks, scratch, flops):
    return pl.pallas_call(
        kernel,
        out_shape=[jax.ShapeDtypeStruct(shape, dtype) for shape, dtype in outs],
        in_specs=[pl.BlockSpec(memory_space=pltpu.SMEM)] + [pl.BlockSpec(memory_space=pltpu.VMEM)] * (blocks + 1),
        scratch_shapes=scratch,
        compiler_params=pltpu.CompilerParams(vmem_limit_bytes=40 * 1024 * 1024),
        cost_estimate=pl.CostEstimate(flops=flops, bytes_accessed=4_000_000, transcendentals=0),
    )


def local(feats_t, w_first, w_second, stale_rows, tile_vals, tile_src, tile_count, labels):
    blk = tile_vals.shape[-1]
    hid = w_first.shape[1]
    classes = w_second.shape[1]
    own = labels.shape[0]
    reach = own + 2 * blk
    n_grp, n_dom = lax.axis_size("grp"), lax.axis_size("dom")
    scale = 1.0 / math.sqrt(own * n_grp * n_dom)
    feat_rows = feats_t.shape[0]
    feat_all = feat_rows * n_dom
    half = hid // 2
    core = lax.axis_index("grp") % 2

    parts = feats_t.reshape(feat_rows, n_dom, own)
    edge = jnp.zeros((feat_rows, 1, blk), BF)
    left = jnp.concatenate([edge, parts[:, :-1, own - blk :]], axis=1)
    right = jnp.concatenate([parts[:, 1:, :blk], edge], axis=1)
    wide = jnp.concatenate([left, parts, right], axis=2)
    wide, tile_vals, stale_rows = lax.optimization_barrier((wide, tile_vals, stale_rows))
    feats = lax.all_to_all(wide, "dom", split_axis=1, concat_axis=0, tiled=True).reshape(feat_all, reach)

    adj = adjacency(tile_vals, tile_src, tile_count, reach // blk + 2)
    stale_rows, adj = lax.optimization_barrier((stale_rows, adj))
    before = from_previous(stale_rows, "grp")
    after = from_next(stale_rows, "grp")
    stale_part = dot(adj[:, reach:], jnp.concatenate([before, after], axis=0), 1, 0)
    mark = (labels[:, None] == jnp.arange(classes, dtype=jnp.int32)[None, :]).astype(F32)

    agg_t, hidden, slope, proj_second = whole(
        forward_kernel,
        [((feat_all, own), BF), ((own, hid), BF), ((own, hid), F32), ((own, classes), BF)],
        flops=2 * own * (2 * feat_all * reach + feat_all * hid + hid * classes),
    )(adj, feats, w_first, stale_part, w_second)

    up = from_previous(proj_second[own - blk :], "dom")
    down = from_next(proj_second[:blk], "dom")
    logits, inner, rim_up, rim_down = whole(
        functools.partial(middle_kernel, hid),
        [((own, classes), BF), ((own, classes), F32), ((blk, classes), BF), ((blk, classes), BF)],
        flops=4 * own * reach * classes,
    )(adj, up, proj_second, down, stale_part, mark)

    to_first = from_previous(rim_down, "dom")
    to_last = from_next(rim_up, "dom")
    width = half + classes
    send, keep, grad_agg = whole_core(
        functools.partial(backward_kernel, scale),
        [((feat_all, width), BF), ((feat_all, width), F32), ((own, hid), BF)],
        6,
        scratch=[pltpu.VMEM((n_dom, 2, feat_rows, classes), F32)],
        flops=2 * own * (hid * classes * 2 + feat_all * hid),
    )(core[None], inner, to_first, to_last, hidden, w_second, slope, agg_t)
    summed = (keep + swapped(send, "grp").astype(F32)).astype(BF)

    (grad_wide,) = whole(
        feature_kernel, [((feat_all, reach), BF)], flops=2 * own * (hid * feat_all + reach * feat_all)
    )(grad_agg, w_first, adj)
    sent = jnp.concatenate([summed, grad_wide], axis=1)
    got = lax.all_to_all(sent, "dom", split_axis=0, concat_axis=0, tiled=True).reshape(n_dom, feat_rows, -1)

    band = jnp.sum(got[:, :, :width].astype(F32), axis=0).astype(BF)
    copies = jnp.broadcast_to(band[None], (n_grp, feat_rows, width))
    bands = lax.all_to_all(copies, "grp", split_axis=0, concat_axis=0, tiled=True)
    total = jnp.sum(bands.reshape(n_grp // 2, 2, feat_rows, width).astype(F32), axis=0)
    grad_first = jnp.concatenate([total[0, :, :half], total[1, :, :half]], axis=1)
    grad_second = total[:, :, half:].reshape(2 * feat_rows, classes)

    wide_back = got[:, :, width:].astype(F32)
    none = jnp.zeros((1, feat_rows, blk), F32)
    first_block = jnp.concatenate([none, wide_back[:-1, :, reach - blk :]], axis=0)
    last_block = jnp.concatenate([wide_back[1:, :, :blk], none], axis=0)
    middle = jnp.zeros((n_dom, feat_rows, own - blk), F32)
    grad_feats = (
        wide_back[:, :, blk : reach - blk]
        + jnp.concatenate([first_block, middle], axis=2)
        + jnp.concatenate([middle, last_block], axis=2)
    )
    grad_feats = grad_feats.astype(BF).transpose(1, 0, 2).reshape(feat_rows, n_dom * own)
    return (logits, grad_feats, grad_first, grad_second)


def solution(mesh):
    return jax.shard_map(
        local,
        mesh=mesh,
        in_specs=(
            P("dom", "grp"),
            P(),
            P(),
            P(("grp", "dom"), None),
            P(("grp", "dom"), None, None, None),
            P(("grp", "dom"), None),
            P(("grp", "dom")),
            P(("grp", "dom")),
        ),
        out_specs=(P(("grp", "dom"), None), P("dom", "grp"), P("dom", None), P("dom", None)),
        check_vma=False,
    )
```

```python
import functools
import math

import jax
import jax.numpy as jnp
from jax import lax
from jax.experimental import pallas as pl
from jax.experimental.pallas import tpu as pltpu
from jax.sharding import PartitionSpec as P

BF = jnp.bfloat16
F32 = jnp.float32


def dot(a, b, ca, cb):
    return lax.dot_general(a, b, (((ca,), (cb,)), ((), ())), preferred_element_type=F32)


def swapped(x, axis):
    count = lax.axis_size(axis)
    return lax.ppermute(x, axis, [(i, i ^ 1) for i in range(count)])


def from_previous(x, axis):
    count = lax.axis_size(axis)
    return lax.ppermute(x, axis, [(i, i + 1) for i in range(count - 1)])


def from_next(x, axis):
    count = lax.axis_size(axis)
    return lax.ppermute(x, axis, [(i + 1, i) for i in range(count - 1)])


def whole(kernel, outs, scratch=(), flops=0):
    return pl.pallas_call(
        kernel,
        out_shape=[jax.ShapeDtypeStruct(shape, dtype) for shape, dtype in outs],
        scratch_shapes=list(scratch),
        compiler_params=pltpu.CompilerParams(vmem_limit_bytes=16 * 1024 * 1024),
        cost_estimate=pl.CostEstimate(flops=flops, bytes_accessed=4_000_000, transcendentals=0),
    )


def widen_kernel(feats, wide):
    parts, rows, reach = wide.shape
    own = feats.shape[1] // parts
    blk = (reach - own) // 2
    none = jnp.zeros((rows, blk), wide.dtype)
    for d in range(parts):
        first, last = d * own - blk, (d + 1) * own + blk
        wide[d, :, blk : blk + own] = feats[:, d * own : (d + 1) * own]
        wide[d, :, :blk] = feats[:, first : first + blk] if d > 0 else none
        wide[d, :, blk + own :] = feats[:, last - blk : last] if d < parts - 1 else none


def adjacency_kernel(src, count, tiles, adj):
    block_rows, slots, blk, _ = tiles.shape
    for r in range(block_rows):
        live = count[r]
        for t in range(adj.shape[1] // blk):
            block = jnp.zeros((blk, blk), BF)
            for k in range(slots):
                hit = jnp.logical_and(src[r, k] == t, k < live)
                block = jnp.where(hit, tiles[r, k], block)
            adj[r * blk : (r + 1) * blk, t * blk : (t + 1) * blk] = block


def total_kernel(bands, first, second):
    cores, half = 2, first.shape[1] // 2
    rows = first.shape[0]
    for c in range(cores):
        total = bands[c].astype(F32)
        for z in range(1, bands.shape[0] // cores):
            total += bands[z * cores + c].astype(F32)
        first[:, c * half : (c + 1) * half] = total[:, :half]
        second[c * rows : (c + 1) * rows, :] = total[:, half:]


def forward_kernel(adj, feats, w_first, stale, w_second, agg_t, hidden, slope, proj):
    width = feats.shape[1]
    hid = w_first.shape[1]
    step = min(256, hid)
    m = adj[:, :width]
    agg = dot(m, feats[...], 1, 1).astype(BF)
    agg_t[...] = dot(feats[...], m, 1, 1).astype(BF)
    total = jnp.zeros(proj.shape, F32)
    for at in range(0, hid, step):
        cols = slice(at, at + step)
        a = dot(agg, w_first[:, cols], 1, 0) + stale[:, cols]
        s = jax.nn.sigmoid(a)
        h = (a * s).astype(BF)
        hidden[:, cols] = h
        slope[:, cols] = s * (1.0 + a * (1.0 - s))
        total += dot(h, w_second[cols, :], 1, 0)
    proj[...] = total.astype(BF)


def middle_kernel(hid, adj, up, own, down, stale, mark, logits, inner, rim_up, rim_down):
    blk = up.shape[0]
    size = own.shape[0]
    reach = size + 2 * blk
    agg = dot(adj[:, :blk], up[...], 1, 0)
    agg += dot(adj[:, blk : blk + size], own[...], 1, 0)
    agg += dot(adj[:, blk + size : reach], down[...], 1, 0)
    agg += stale[:, hid:]
    logits[...] = agg.astype(BF)
    e = jnp.exp(agg - jnp.max(agg, axis=1, keepdims=True))
    grad = (e / jnp.sum(e, axis=1, keepdims=True) - mark[...]).astype(BF)
    spread = dot(adj[:, :reach], grad, 0, 0)
    inner[...] = spread[blk : blk + size]
    rim_up[...] = spread[:blk].astype(BF)
    rim_down[...] = spread[blk + size :].astype(BF)


def backward_kernel(scale, core, inner, up, down, hidden, w_second, slope, agg_t, send, keep, grad_agg, second):
    blk = up.shape[0]
    size = inner.shape[0]
    hid = slope.shape[1]
    step = min(256, hid)
    half = hid // 2
    other = 1 - core[0]
    upper = inner[:blk] + up[...].astype(F32)
    lower = inner[size - blk :] + down[...].astype(F32)
    if size > 2 * blk:
        parts = [upper, inner[blk : size - blk], lower]
    else:
        parts = [upper, lower]
    grad_p2 = jnp.concatenate(parts, axis=0).astype(BF)
    for at in range(0, hid, step):
        cols = slice(at, at + step)
        grad_agg[:, cols] = (dot(grad_p2, w_second[cols, :], 1, 1) * slope[:, cols]).astype(BF)
    second[...] = (dot(hidden[...], grad_p2, 0, 0) * scale).reshape(second.shape)
    rows = second.shape[0] * second.shape[2]
    send[:, half:] = second[:, other].reshape(rows, second.shape[3]).astype(BF)
    keep[:, half:] = second[:, core[0]].reshape(rows, second.shape[3])
    for mine, out in ((other, send), (core[0], keep)):
        g = grad_agg[:, pl.ds(pl.multiple_of(mine * half, half), half)]
        out[:, :half] = (dot(agg_t[...], g, 1, 0) * scale).astype(out.dtype)


def feature_kernel(grad_agg, w_first, adj, out):
    width = out.shape[1]
    back = dot(w_first[...], grad_agg[...], 1, 1).astype(BF)
    out[...] = dot(back, adj[:, :width], 1, 0).astype(BF)


def whole_core(kernel, outs, blocks, scratch=(), flops=0, scalars=1):
    return pl.pallas_call(
        kernel,
        out_shape=[jax.ShapeDtypeStruct(shape, dtype) for shape, dtype in outs],
        in_specs=[pl.BlockSpec(memory_space=pltpu.SMEM)] * scalars + [pl.BlockSpec(memory_space=pltpu.VMEM)] * blocks,
        scratch_shapes=scratch,
        compiler_params=pltpu.CompilerParams(vmem_limit_bytes=16 * 1024 * 1024),
        cost_estimate=pl.CostEstimate(flops=flops, bytes_accessed=4_000_000, transcendentals=0),
    )


def local(feats_t, w_first, w_second, stale_rows, tile_vals, tile_src, tile_count, labels):
    blk = tile_vals.shape[-1]
    hid = w_first.shape[1]
    classes = w_second.shape[1]
    own = labels.shape[0]
    reach = own + 2 * blk
    n_grp, n_dom = lax.axis_size("grp"), lax.axis_size("dom")
    scale = 1.0 / math.sqrt(own * n_grp * n_dom)
    feat_rows = feats_t.shape[0]
    feat_all = feat_rows * n_dom
    half = hid // 2
    core = lax.axis_index("grp") % 2

    (wide,) = whole(widen_kernel, [((n_dom, feat_rows, reach), BF)])(feats_t)
    wide, tile_vals, stale_rows = lax.optimization_barrier((wide, tile_vals, stale_rows))
    feats = lax.all_to_all(wide, "dom", split_axis=0, concat_axis=0, tiled=True).reshape(feat_all, reach)

    (adj,) = whole_core(adjacency_kernel, [((own, reach + 2 * blk), BF)], 1, scalars=2)(
        tile_src, tile_count, tile_vals
    )
    stale_rows, adj = lax.optimization_barrier((stale_rows, adj))
    before = from_previous(stale_rows, "grp")
    after = from_next(stale_rows, "grp")
    stale_part = dot(adj[:, reach:], jnp.concatenate([before, after], axis=0), 1, 0)
    mark = (labels[:, None] == jnp.arange(classes, dtype=jnp.int32)[None, :]).astype(F32)

    agg_t, hidden, slope, proj_second = whole(
        forward_kernel,
        [((feat_all, own), BF), ((own, hid), BF), ((own, hid), F32), ((own, classes), BF)],
        flops=2 * own * (2 * feat_all * reach + feat_all * hid + hid * classes),
    )(adj, feats, w_first, stale_part, w_second)

    up = from_previous(proj_second[own - blk :], "dom")
    down = from_next(proj_second[:blk], "dom")
    logits, inner, rim_up, rim_down = whole(
        functools.partial(middle_kernel, hid),
        [((own, classes), BF), ((own, classes), F32), ((blk, classes), BF), ((blk, classes), BF)],
        flops=4 * own * reach * classes,
    )(adj, up, proj_second, down, stale_part, mark)

    to_first = from_previous(rim_down, "dom")
    to_last = from_next(rim_up, "dom")
    width = half + classes
    send, keep, grad_agg = whole_core(
        functools.partial(backward_kernel, scale),
        [((feat_all, width), BF), ((feat_all, width), F32), ((own, hid), BF)],
        7,
        scratch=[pltpu.VMEM((n_dom, 2, feat_rows, classes), F32)],
        flops=2 * own * (hid * classes * 2 + feat_all * hid),
    )(core[None], inner, to_first, to_last, hidden, w_second, slope, agg_t)
    summed = (keep + swapped(send, "grp").astype(F32)).astype(BF)

    (grad_wide,) = whole(
        feature_kernel, [((feat_all, reach), BF)], flops=2 * own * (hid * feat_all + reach * feat_all)
    )(grad_agg, w_first, adj)
    sent = jnp.concatenate([summed, grad_wide], axis=1)
    got = lax.all_to_all(sent, "dom", split_axis=0, concat_axis=0, tiled=True).reshape(n_dom, feat_rows, -1)

    band = jnp.sum(got[:, :, :width].astype(F32), axis=0).astype(BF)
    copies = jnp.broadcast_to(band[None], (n_grp, feat_rows, width))
    bands = lax.all_to_all(copies, "grp", split_axis=0, concat_axis=0, tiled=True)
    grad_first, grad_second = whole(
        total_kernel, [((feat_rows, hid), F32), ((2 * feat_rows, classes), F32)]
    )(bands)

    wide_back = got[:, :, width:].astype(F32)
    none = jnp.zeros((1, feat_rows, blk), F32)
    first_block = jnp.concatenate([none, wide_back[:-1, :, reach - blk :]], axis=0)
    last_block = jnp.concatenate([wide_back[1:, :, :blk], none], axis=0)
    middle = jnp.zeros((n_dom, feat_rows, own - blk), F32)
    grad_feats = (
        wide_back[:, :, blk : reach - blk]
        + jnp.concatenate([first_block, middle], axis=2)
        + jnp.concatenate([middle, last_block], axis=2)
    )
    grad_feats = grad_feats.astype(BF).transpose(1, 0, 2).reshape(feat_rows, n_dom * own)
    return (logits, grad_feats, grad_first, grad_second)


def solution(mesh):
    return jax.shard_map(
        local,
        mesh=mesh,
        in_specs=(
            P("dom", "grp"),
            P(),
            P(),
            P(("grp", "dom"), None),
            P(("grp", "dom"), None, None, None),
            P(("grp", "dom"), None),
            P(("grp", "dom")),
            P(("grp", "dom")),
        ),
        out_specs=(P(("grp", "dom"), None), P("dom", "grp"), P("dom", None), P("dom", None)),
        check_vma=False,
    )
```

```python
import functools
import math

import jax
import jax.numpy as jnp
from jax import lax
from jax.experimental import pallas as pl
from jax.experimental.pallas import tpu as pltpu
from jax.sharding import PartitionSpec as P

BF = jnp.bfloat16
F32 = jnp.float32


def dot(a, b, ca, cb):
    return lax.dot_general(a, b, (((ca,), (cb,)), ((), ())), preferred_element_type=F32)


def swapped(x, axis):
    count = lax.axis_size(axis)
    return lax.ppermute(x, axis, [(i, i ^ 1) for i in range(count)])


def from_previous(x, axis):
    count = lax.axis_size(axis)
    return lax.ppermute(x, axis, [(i, i + 1) for i in range(count - 1)])


def from_next(x, axis):
    count = lax.axis_size(axis)
    return lax.ppermute(x, axis, [(i + 1, i) for i in range(count - 1)])


def paired(x, axis, first):
    count = lax.axis_size(axis)
    pairs = []
    for i in range(first, count - 1, 2):
        pairs += [(i, i + 1), (i + 1, i)]
    return lax.ppermute(x, axis, pairs)


def whole(kernel, outs, scratch=(), flops=0):
    return pl.pallas_call(
        kernel,
        out_shape=[jax.ShapeDtypeStruct(shape, dtype) for shape, dtype in outs],
        scratch_shapes=list(scratch),
        compiler_params=pltpu.CompilerParams(vmem_limit_bytes=16 * 1024 * 1024),
        cost_estimate=pl.CostEstimate(flops=flops, bytes_accessed=4_000_000, transcendentals=0),
    )


def widen_kernel(feats, wide, none, sems):
    parts, _, reach = wide.shape
    own = feats.shape[1] // parts
    blk = (reach - own) // 2
    none[...] = jnp.zeros_like(none)
    copies = []
    for d in range(parts):
        low, high = max(d * own - blk, 0), min((d + 1) * own + blk, parts * own)
        start = low - (d * own - blk)
        copies.append((feats.at[:, low:high], wide.at[d, :, start : start + high - low]))
    copies.append((none, wide.at[0, :, :blk]))
    copies.append((none, wide.at[parts - 1, :, reach - blk :]))
    copies = [pltpu.make_async_copy(src, dst, sems.at[i]) for i, (src, dst) in enumerate(copies)]
    for copy in copies:
        copy.start()
    for copy in copies:
        copy.wait()


def adjacency_kernel(src, count, tiles, adj):
    block_rows, slots, blk, _ = tiles.shape
    for r in range(block_rows):
        live = count[r]
        for t in range(adj.shape[1] // blk):
            block = jnp.zeros((blk, blk), BF)
            for k in range(slots):
                hit = jnp.logical_and(src[r, k] == t, k < live)
                block = jnp.where(hit, tiles[r, k], block)
            adj[r * blk : (r + 1) * blk, t * blk : (t + 1) * blk] = block


def total_kernel(bands, first, second):
    cores, half = 2, first.shape[1] // 2
    rows = first.shape[0]
    for c in range(cores):
        total = bands[c].astype(F32)
        for z in range(1, bands.shape[0] // cores):
            total += bands[z * cores + c].astype(F32)
        first[:, c * half : (c + 1) * half] = total[:, :half]
        second[c * rows : (c + 1) * rows, :] = total[:, half:]


def forward_kernel(odd, adj, feats, w_first, stale, w_second, agg_t, hidden, slope, proj, within, across):
    width = feats.shape[1]
    hid = w_first.shape[1]
    step = min(256, hid)
    m = adj[:, :width]
    agg = dot(m, feats[...], 1, 1).astype(BF)
    agg_t[...] = dot(feats[...], m, 1, 1).astype(BF)
    total = jnp.zeros(proj.shape, F32)
    for at in range(0, hid, step):
        cols = slice(at, at + step)
        a = dot(agg, w_first[:, cols], 1, 0) + stale[:, cols]
        s = jax.nn.sigmoid(a)
        h = (a * s).astype(BF)
        hidden[:, cols] = h
        slope[:, cols] = s * (1.0 + a * (1.0 - s))
        total += dot(h, w_second[cols, :], 1, 0)
    proj[...] = total.astype(BF)
    blk = within.shape[0]
    top, bottom = proj[:blk], proj[proj.shape[0] - blk :]
    is_odd = odd[0] == 1
    within[...] = jnp.where(is_odd, top, bottom)
    across[...] = jnp.where(is_odd, bottom, top)


def middle_kernel(
    hid, odd, adj, own, paired_in, crossed_in, stale, mark, _hidden, _slope, _agg_t, logits, inner, within, across
):
    blk = within.shape[0]
    is_odd = odd[0] == 1
    up = jnp.where(is_odd, paired_in[...], crossed_in[...])
    down = jnp.where(is_odd, crossed_in[...], paired_in[...])
    size = own.shape[0]
    reach = size + 2 * blk
    agg = dot(adj[:, :blk], up, 1, 0)
    agg += dot(adj[:, blk : blk + size], own[...], 1, 0)
    agg += dot(adj[:, blk + size : reach], down, 1, 0)
    agg += stale[:, hid:]
    logits[...] = agg.astype(BF)
    e = jnp.exp(agg - jnp.max(agg, axis=1, keepdims=True))
    grad = (e / jnp.sum(e, axis=1, keepdims=True) - mark[...]).astype(BF)
    spread = dot(adj[:, :reach], grad, 0, 0)
    inner[...] = spread[blk : blk + size]
    rim_up, rim_down = spread[:blk], spread[blk + size :]
    within[...] = jnp.where(is_odd, rim_up, rim_down).astype(BF)
    across[...] = jnp.where(is_odd, rim_down, rim_up).astype(BF)


def backward_kernel(
    scale, odd, core, inner, paired_in, crossed_in, hidden, w_second, slope, agg_t, send, kept, grad_agg, second
):
    blk = paired_in.shape[0]
    size = inner.shape[0]
    hid = slope.shape[1]
    step = min(256, hid)
    half = hid // 2
    is_odd = odd[0] == 1
    mine, other = core[0], 1 - core[0]
    upper = inner[:blk] + jnp.where(is_odd, paired_in[...], crossed_in[...]).astype(F32)
    lower = inner[size - blk :] + jnp.where(is_odd, crossed_in[...], paired_in[...]).astype(F32)
    if size > 2 * blk:
        parts = [upper, inner[blk : size - blk], lower]
    else:
        parts = [upper, lower]
    grad_p2 = jnp.concatenate(parts, axis=0).astype(BF)
    for at in range(0, hid, step):
        cols = slice(at, at + step)
        grad_agg[:, cols] = (dot(grad_p2, w_second[cols, :], 1, 1) * slope[:, cols]).astype(BF)
    second[...] = (dot(hidden[...], grad_p2, 0, 0) * scale).reshape(second.shape)
    rows = second.shape[0] * second.shape[2]
    send[:, half:] = second[:, other].reshape(rows, second.shape[3]).astype(BF)
    kept[...] = second[:, mine].reshape(rows, second.shape[3])
    g = grad_agg[:, pl.ds(pl.multiple_of(other * half, half), half)]
    send[:, :half] = (dot(agg_t[...], g, 1, 0) * scale).astype(BF)


def feature_kernel(scale, core, grad_agg, w_first, adj, agg_t, kept, keep, out):
    width = out.shape[1]
    half = grad_agg.shape[1] // 2
    g = grad_agg[:, pl.ds(pl.multiple_of(core[0] * half, half), half)]
    keep[:, :half] = dot(agg_t[...], g, 1, 0) * scale
    keep[:, half:] = kept[...]
    back = dot(w_first[...], grad_agg[...], 1, 1).astype(BF)
    out[...] = dot(back, adj[:, :width], 1, 0).astype(BF)


def whole_core(kernel, outs, blocks, scratch=(), flops=0, scalars=1):
    return pl.pallas_call(
        kernel,
        out_shape=[jax.ShapeDtypeStruct(shape, dtype) for shape, dtype in outs],
        in_specs=[pl.BlockSpec(memory_space=pltpu.SMEM)] * scalars + [pl.BlockSpec(memory_space=pltpu.VMEM)] * blocks,
        scratch_shapes=scratch,
        compiler_params=pltpu.CompilerParams(vmem_limit_bytes=16 * 1024 * 1024),
        cost_estimate=pl.CostEstimate(flops=flops, bytes_accessed=4_000_000, transcendentals=0),
    )


def local(feats_t, w_first, w_second, stale_rows, tile_vals, tile_src, tile_count, labels):
    blk = tile_vals.shape[-1]
    hid = w_first.shape[1]
    classes = w_second.shape[1]
    own = labels.shape[0]
    reach = own + 2 * blk
    n_grp, n_dom = lax.axis_size("grp"), lax.axis_size("dom")
    scale = 1.0 / math.sqrt(own * n_grp * n_dom)
    feat_rows = feats_t.shape[0]
    feat_all = feat_rows * n_dom
    half = hid // 2
    core = lax.axis_index("grp") % 2

    wide = pl.pallas_call(
        widen_kernel,
        out_shape=jax.ShapeDtypeStruct((n_dom, feat_rows, reach), BF),
        in_specs=[pl.BlockSpec(memory_space=pl.ANY)],
        out_specs=pl.BlockSpec(memory_space=pl.ANY),
        scratch_shapes=[pltpu.VMEM((feat_rows, blk), BF), pltpu.SemaphoreType.DMA((n_dom + 2,))],
        cost_estimate=pl.CostEstimate(flops=0, bytes_accessed=1_000_000, transcendentals=0),
    )(feats_t)
    wide, tile_vals, stale_rows = lax.optimization_barrier((wide, tile_vals, stale_rows))
    feats = lax.all_to_all(wide, "dom", split_axis=0, concat_axis=0, tiled=True).reshape(feat_all, reach)

    (adj,) = whole_core(adjacency_kernel, [((own, reach + 2 * blk), BF)], 1, scalars=2)(
        tile_src, tile_count, tile_vals
    )
    stale_rows, adj = lax.optimization_barrier((stale_rows, adj))
    before = from_previous(stale_rows, "grp")
    after = from_next(stale_rows, "grp")
    stale_part = dot(adj[:, reach:], jnp.concatenate([before, after], axis=0), 1, 0)
    mark = (labels[:, None] == jnp.arange(classes, dtype=jnp.int32)[None, :]).astype(F32)

    odd = (lax.axis_index("dom") % 2)[None]
    agg_t, hidden, slope, proj_second, within, across = whole_core(
        forward_kernel,
        [
            ((feat_all, own), BF),
            ((own, hid), BF),
            ((own, hid), F32),
            ((own, classes), BF),
            ((blk, classes), BF),
            ((blk, classes), BF),
        ],
        5,
        flops=2 * own * (2 * feat_all * reach + feat_all * hid + hid * classes),
    )(odd, adj, feats, w_first, stale_part, w_second)

    logits, inner, within, across = whole_core(
        functools.partial(middle_kernel, hid),
        [((own, classes), BF), ((own, classes), F32), ((blk, classes), BF), ((blk, classes), BF)],
        9,
        flops=4 * own * reach * classes,
    )(
        odd,
        adj,
        proj_second,
        paired(within, "dom", 0),
        paired(across, "dom", 1),
        stale_part,
        mark,
        hidden,
        slope,
        agg_t,
    )

    width = half + classes
    send, kept, grad_agg = whole_core(
        functools.partial(backward_kernel, scale),
        [((feat_all, width), BF), ((feat_all, classes), F32), ((own, hid), BF)],
        7,
        scratch=[pltpu.VMEM((n_dom, 2, feat_rows, classes), F32)],
        flops=2 * own * (hid * classes * 2 + feat_all * half),
        scalars=2,
    )(odd, core[None], inner, paired(within, "dom", 0), paired(across, "dom", 1), hidden, w_second, slope, agg_t)
    received = swapped(send, "grp")

    keep, grad_wide = whole_core(
        functools.partial(feature_kernel, scale),
        [((feat_all, width), F32), ((feat_all, reach), BF)],
        5,
        flops=2 * own * (hid * feat_all + reach * feat_all + feat_all * half),
    )(core[None], grad_agg, w_first, adj, agg_t, kept)
    summed = (keep + received.astype(F32)).astype(BF)
    sent = jnp.concatenate([summed, grad_wide], axis=1)
    got = lax.all_to_all(sent, "dom", split_axis=0, concat_axis=0, tiled=True).reshape(n_dom, feat_rows, -1)

    band = jnp.sum(got[:, :, :width].astype(F32), axis=0).astype(BF)
    copies = jnp.broadcast_to(band[None], (n_grp, feat_rows, width))
    bands = lax.all_to_all(copies, "grp", split_axis=0, concat_axis=0, tiled=True)
    grad_first, grad_second = whole(
        total_kernel, [((feat_rows, hid), F32), ((2 * feat_rows, classes), F32)]
    )(bands)

    wide_back = got[:, :, width:].astype(F32)
    none = jnp.zeros((1, feat_rows, blk), F32)
    first_block = jnp.concatenate([none, wide_back[:-1, :, reach - blk :]], axis=0)
    last_block = jnp.concatenate([wide_back[1:, :, :blk], none], axis=0)
    middle = jnp.zeros((n_dom, feat_rows, own - blk), F32)
    grad_feats = (
        wide_back[:, :, blk : reach - blk]
        + jnp.concatenate([first_block, middle], axis=2)
        + jnp.concatenate([middle, last_block], axis=2)
    )
    grad_feats = grad_feats.astype(BF).transpose(1, 0, 2).reshape(feat_rows, n_dom * own)
    return (logits, grad_feats, grad_first, grad_second)


def solution(mesh):
    return jax.shard_map(
        local,
        mesh=mesh,
        in_specs=(
            P("dom", "grp"),
            P(),
            P(),
            P(("grp", "dom"), None),
            P(("grp", "dom"), None, None, None),
            P(("grp", "dom"), None),
            P(("grp", "dom")),
            P(("grp", "dom")),
        ),
        out_specs=(P(("grp", "dom"), None), P("dom", "grp"), P("dom", None), P("dom", None)),
        check_vma=False,
    )
```

```python
import functools
import math

import jax
import jax.numpy as jnp
from jax import lax
from jax.experimental import pallas as pl
from jax.experimental.pallas import tpu as pltpu
from jax.sharding import PartitionSpec as P

BF = jnp.bfloat16
F32 = jnp.float32


def dot(a, b, ca, cb):
    return lax.dot_general(a, b, (((ca,), (cb,)), ((), ())), preferred_element_type=F32)


def swapped(x, axis):
    count = lax.axis_size(axis)
    return lax.ppermute(x, axis, [(i, i ^ 1) for i in range(count)])


def from_previous(x, axis):
    count = lax.axis_size(axis)
    return lax.ppermute(x, axis, [(i, i + 1) for i in range(count - 1)])


def from_next(x, axis):
    count = lax.axis_size(axis)
    return lax.ppermute(x, axis, [(i + 1, i) for i in range(count - 1)])


def paired(x, axis, first):
    count = lax.axis_size(axis)
    pairs = []
    for i in range(first, count - 1, 2):
        pairs += [(i, i + 1), (i + 1, i)]
    return lax.ppermute(x, axis, pairs)


def here(x):
    return pltpu.with_memory_space_constraint(x, pltpu.VMEM)


def result(shape, dtype, keep=False):
    return pltpu.VMEM(shape, dtype) if keep else jax.ShapeDtypeStruct(shape, dtype)


def whole(kernel, outs, scratch=(), flops=0):
    return pl.pallas_call(
        kernel,
        out_shape=[result(*out) for out in outs],
        scratch_shapes=list(scratch),
        compiler_params=pltpu.CompilerParams(vmem_limit_bytes=16 * 1024 * 1024),
        cost_estimate=pl.CostEstimate(flops=flops, bytes_accessed=4_000_000, transcendentals=0),
    )


def widen_kernel(feats, wide):
    parts, rows, reach = wide.shape
    own = feats.shape[1] // parts
    blk = (reach - own) // 2
    none = jnp.zeros((rows, blk), wide.dtype)
    for d in range(parts):
        first, last = d * own - blk, (d + 1) * own + blk
        wide[d, :, blk : blk + own] = feats[:, d * own : (d + 1) * own]
        wide[d, :, :blk] = feats[:, first : first + blk] if d > 0 else none
        wide[d, :, blk + own :] = feats[:, last - blk : last] if d < parts - 1 else none


def adjacency_kernel(src, count, tiles, adj):
    block_rows, slots, blk, _ = tiles.shape
    for r in range(block_rows):
        live = count[r]
        for t in range(adj.shape[1] // blk):
            block = jnp.zeros((blk, blk), BF)
            for k in range(slots):
                hit = jnp.logical_and(src[r, k] == t, k < live)
                block = jnp.where(hit, tiles[r, k], block)
            adj[r * blk : (r + 1) * blk, t * blk : (t + 1) * blk] = block


def stale_kernel(adj, before, after, out):
    rows = before.shape[0]
    at = adj.shape[1] - 2 * rows
    out[...] = dot(adj[:, at : at + rows], before[...], 1, 0) + dot(adj[:, at + rows :], after[...], 1, 0)


def total_kernel(bands, first, second):
    cores, half = 2, first.shape[1] // 2
    rows = first.shape[0]
    for c in range(cores):
        total = bands[c].astype(F32)
        for z in range(1, bands.shape[0] // cores):
            total += bands[z * cores + c].astype(F32)
        first[:, c * half : (c + 1) * half] = total[:, :half]
        second[c * rows : (c + 1) * rows, :] = total[:, half:]


def forward_kernel(odd, adj, feats, w_first, stale, w_second, agg_t, hidden, slope, proj, within, across):
    width = feats.shape[1]
    hid = w_first.shape[1]
    step = min(256, hid)
    m = adj[:, :width]
    agg = dot(m, feats[...], 1, 1).astype(BF)
    agg_t[...] = dot(feats[...], m, 1, 1).astype(BF)
    total = jnp.zeros(proj.shape, F32)
    for at in range(0, hid, step):
        cols = slice(at, at + step)
        a = dot(agg, w_first[:, cols], 1, 0) + stale[:, cols]
        s = jax.nn.sigmoid(a)
        h = (a * s).astype(BF)
        hidden[:, cols] = h
        slope[:, cols] = s * (1.0 + a * (1.0 - s))
        total += dot(h, w_second[cols, :], 1, 0)
    proj[...] = total.astype(BF)
    blk = within.shape[0]
    top, bottom = proj[:blk], proj[proj.shape[0] - blk :]
    is_odd = odd[0] == 1
    within[...] = jnp.where(is_odd, top, bottom)
    across[...] = jnp.where(is_odd, bottom, top)


def middle_kernel(
    hid, odd, adj, own, paired_in, crossed_in, stale, mark, logits, inner, within, across
):
    blk = within.shape[0]
    is_odd = odd[0] == 1
    up = jnp.where(is_odd, paired_in[...], crossed_in[...])
    down = jnp.where(is_odd, crossed_in[...], paired_in[...])
    size = own.shape[0]
    reach = size + 2 * blk
    agg = dot(adj[:, :blk], up, 1, 0)
    agg += dot(adj[:, blk : blk + size], own[...], 1, 0)
    agg += dot(adj[:, blk + size : reach], down, 1, 0)
    agg += stale[:, hid:]
    logits[...] = agg.astype(BF)
    e = jnp.exp(agg - jnp.max(agg, axis=1, keepdims=True))
    grad = (e / jnp.sum(e, axis=1, keepdims=True) - mark[...]).astype(BF)
    spread = dot(adj[:, :reach], grad, 0, 0)
    inner[...] = spread[blk : blk + size]
    rim_up, rim_down = spread[:blk], spread[blk + size :]
    within[...] = jnp.where(is_odd, rim_up, rim_down).astype(BF)
    across[...] = jnp.where(is_odd, rim_down, rim_up).astype(BF)


def backward_kernel(
    scale, odd, core, inner, paired_in, crossed_in, hidden, w_second, slope, agg_t, send, kept, grad_agg, second
):
    blk = paired_in.shape[0]
    size = inner.shape[0]
    hid = slope.shape[1]
    step = min(256, hid)
    half = hid // 2
    is_odd = odd[0] == 1
    mine, other = core[0], 1 - core[0]
    upper = inner[:blk] + jnp.where(is_odd, paired_in[...], crossed_in[...]).astype(F32)
    lower = inner[size - blk :] + jnp.where(is_odd, crossed_in[...], paired_in[...]).astype(F32)
    if size > 2 * blk:
        parts = [upper, inner[blk : size - blk], lower]
    else:
        parts = [upper, lower]
    grad_p2 = jnp.concatenate(parts, axis=0).astype(BF)
    for at in range(0, hid, step):
        cols = slice(at, at + step)
        grad_agg[:, cols] = (dot(grad_p2, w_second[cols, :], 1, 1) * slope[:, cols]).astype(BF)
    second[...] = (dot(hidden[...], grad_p2, 0, 0) * scale).reshape(second.shape)
    rows = second.shape[0] * second.shape[2]
    send[:, half:] = second[:, other].reshape(rows, second.shape[3]).astype(BF)
    kept[...] = second[:, mine].reshape(rows, second.shape[3])
    g = grad_agg[:, pl.ds(pl.multiple_of(other * half, half), half)]
    send[:, :half] = (dot(agg_t[...], g, 1, 0) * scale).astype(BF)


def feature_kernel(scale, core, grad_agg, w_first, adj, agg_t, kept, keep, out):
    width = out.shape[1]
    half = grad_agg.shape[1] // 2
    g = grad_agg[:, pl.ds(pl.multiple_of(core[0] * half, half), half)]
    keep[:, :half] = dot(agg_t[...], g, 1, 0) * scale
    keep[:, half:] = kept[...]
    back = dot(w_first[...], grad_agg[...], 1, 1).astype(BF)
    out[...] = dot(back, adj[:, :width], 1, 0).astype(BF)


def whole_core(kernel, outs, blocks, scratch=(), flops=0, scalars=1):
    return pl.pallas_call(
        kernel,
        out_shape=[result(*out) for out in outs],
        in_specs=[pl.BlockSpec(memory_space=pltpu.SMEM)] * scalars + [pl.BlockSpec(memory_space=pltpu.VMEM)] * blocks,
        scratch_shapes=scratch,
        compiler_params=pltpu.CompilerParams(vmem_limit_bytes=16 * 1024 * 1024),
        cost_estimate=pl.CostEstimate(flops=flops, bytes_accessed=4_000_000, transcendentals=0),
    )


def local(feats_t, w_first, w_second, stale_rows, tile_vals, tile_src, tile_count, labels):
    blk = tile_vals.shape[-1]
    hid = w_first.shape[1]
    classes = w_second.shape[1]
    own = labels.shape[0]
    reach = own + 2 * blk
    n_grp, n_dom = lax.axis_size("grp"), lax.axis_size("dom")
    scale = 1.0 / math.sqrt(own * n_grp * n_dom)
    feat_rows = feats_t.shape[0]
    feat_all = feat_rows * n_dom
    half = hid // 2
    core = lax.axis_index("grp") % 2

    (wide,) = whole(widen_kernel, [((n_dom, feat_rows, reach), BF)])(feats_t)
    wide, tile_vals, stale_rows = lax.optimization_barrier((wide, tile_vals, stale_rows))
    feats = lax.all_to_all(wide, "dom", split_axis=0, concat_axis=0, tiled=True).reshape(feat_all, reach)

    (adj,) = whole_core(adjacency_kernel, [((own, reach + 2 * blk), BF)], 1, scalars=2)(
        tile_src, tile_count, tile_vals
    )
    stale_rows, adj = lax.optimization_barrier((stale_rows, adj))
    before = from_previous(stale_rows, "grp")
    after = from_next(stale_rows, "grp")
    (stale_part,) = whole(
        stale_kernel, [((own, hid + classes), F32, True)], flops=2 * own * 2 * blk * (hid + classes)
    )(adj, before, after)
    mark = (labels[:, None] == jnp.arange(classes, dtype=jnp.int32)[None, :]).astype(F32)

    odd = (lax.axis_index("dom") % 2)[None]
    agg_t, hidden, slope, proj_second, within, across = whole_core(
        forward_kernel,
        [
            ((feat_all, own), BF, True),
            ((own, hid), BF, True),
            ((own, hid), F32, True),
            ((own, classes), BF),
            ((blk, classes), BF),
            ((blk, classes), BF),
        ],
        5,
        flops=2 * own * (2 * feat_all * reach + feat_all * hid + hid * classes),
    )(odd, adj, feats, w_first, here(stale_part), w_second)

    logits, inner, within, across = whole_core(
        functools.partial(middle_kernel, hid),
        [((own, classes), BF), ((own, classes), F32), ((blk, classes), BF), ((blk, classes), BF)],
        6,
        flops=4 * own * reach * classes,
    )(
        odd,
        adj,
        proj_second,
        paired(within, "dom", 0),
        paired(across, "dom", 1),
        here(stale_part),
        mark,
    )

    width = half + classes
    send, kept, grad_agg = whole_core(
        functools.partial(backward_kernel, scale),
        [((feat_all, width), BF), ((feat_all, classes), F32), ((own, hid), BF)],
        7,
        scratch=[pltpu.VMEM((n_dom, 2, feat_rows, classes), F32)],
        flops=2 * own * (hid * classes * 2 + feat_all * half),
        scalars=2,
    )(odd, core[None], inner, paired(within, "dom", 0), paired(across, "dom", 1), here(hidden), w_second, here(slope), here(agg_t))
    received = swapped(send, "grp")

    keep, grad_wide = whole_core(
        functools.partial(feature_kernel, scale),
        [((feat_all, width), F32), ((feat_all, reach), BF)],
        5,
        flops=2 * own * (hid * feat_all + reach * feat_all + feat_all * half),
    )(core[None], grad_agg, w_first, adj, here(agg_t), kept)
    summed = (keep + received.astype(F32)).astype(BF)
    sent = jnp.concatenate([summed, grad_wide], axis=1)
    got = lax.all_to_all(sent, "dom", split_axis=0, concat_axis=0, tiled=True).reshape(n_dom, feat_rows, -1)

    band = jnp.sum(got[:, :, :width].astype(F32), axis=0).astype(BF)
    copies = jnp.broadcast_to(band[None], (n_grp, feat_rows, width))
    bands = lax.all_to_all(copies, "grp", split_axis=0, concat_axis=0, tiled=True)
    grad_first, grad_second = whole(
        total_kernel, [((feat_rows, hid), F32), ((2 * feat_rows, classes), F32)]
    )(bands)

    wide_back = got[:, :, width:].astype(F32)
    none = jnp.zeros((1, feat_rows, blk), F32)
    first_block = jnp.concatenate([none, wide_back[:-1, :, reach - blk :]], axis=0)
    last_block = jnp.concatenate([wide_back[1:, :, :blk], none], axis=0)
    middle = jnp.zeros((n_dom, feat_rows, own - blk), F32)
    grad_feats = (
        wide_back[:, :, blk : reach - blk]
        + jnp.concatenate([first_block, middle], axis=2)
        + jnp.concatenate([middle, last_block], axis=2)
    )
    grad_feats = grad_feats.astype(BF).transpose(1, 0, 2).reshape(feat_rows, n_dom * own)
    return (logits, grad_feats, grad_first, grad_second)


def solution(mesh):
    return jax.shard_map(
        local,
        mesh=mesh,
        in_specs=(
            P("dom", "grp"),
            P(),
            P(),
            P(("grp", "dom"), None),
            P(("grp", "dom"), None, None, None),
            P(("grp", "dom"), None),
            P(("grp", "dom")),
            P(("grp", "dom")),
        ),
        out_specs=(P(("grp", "dom"), None), P("dom", "grp"), P("dom", None), P("dom", None)),
        check_vma=False,
    )
```

```python
import functools
import math

import jax
import jax.numpy as jnp
from jax import lax
from jax.experimental import pallas as pl
from jax.experimental.pallas import tpu as pltpu
from jax.sharding import PartitionSpec as P

BF = jnp.bfloat16
F32 = jnp.float32


def dot(a, b, ca, cb):
    return lax.dot_general(a, b, (((ca,), (cb,)), ((), ())), preferred_element_type=F32)


def swapped(x, axis):
    count = lax.axis_size(axis)
    return lax.ppermute(x, axis, [(i, i ^ 1) for i in range(count)])


def from_previous(x, axis):
    count = lax.axis_size(axis)
    return lax.ppermute(x, axis, [(i, i + 1) for i in range(count - 1)])


def from_next(x, axis):
    count = lax.axis_size(axis)
    return lax.ppermute(x, axis, [(i + 1, i) for i in range(count - 1)])


def paired(x, axis, first):
    count = lax.axis_size(axis)
    pairs = []
    for i in range(first, count - 1, 2):
        pairs += [(i, i + 1), (i + 1, i)]
    return lax.ppermute(x, axis, pairs)


def in_hbm(x):
    return pltpu.with_memory_space_constraint(x, pltpu.HBM)


def whole(kernel, outs, scratch=(), flops=0):
    return pl.pallas_call(
        kernel,
        out_shape=[jax.ShapeDtypeStruct(*out) for out in outs],
        scratch_shapes=list(scratch),
        compiler_params=pltpu.CompilerParams(vmem_limit_bytes=16 * 1024 * 1024),
        cost_estimate=pl.CostEstimate(flops=flops, bytes_accessed=4_000_000, transcendentals=0),
    )


def widen_kernel(feats, wide):
    parts, rows, reach = wide.shape
    own = feats.shape[1] // parts
    blk = (reach - own) // 2
    none = jnp.zeros((rows, blk), wide.dtype)
    for d in range(parts):
        first, last = d * own - blk, (d + 1) * own + blk
        wide[d, :, blk : blk + own] = feats[:, d * own : (d + 1) * own]
        wide[d, :, :blk] = feats[:, first : first + blk] if d > 0 else none
        wide[d, :, blk + own :] = feats[:, last - blk : last] if d < parts - 1 else none


def adjacency_kernel(src, count, tiles, adj, adj_stale):
    block_rows, slots, blk, _ = tiles.shape
    for r in range(block_rows):
        live = count[r]
        inside = adj.shape[1] // blk
        for t in range(inside + adj_stale.shape[1] // blk):
            block = jnp.zeros((blk, blk), BF)
            for k in range(slots):
                hit = jnp.logical_and(src[r, k] == t, k < live)
                block = jnp.where(hit, tiles[r, k], block)
            out, at = (adj, t) if t < inside else (adj_stale, t - inside)
            out[r * blk : (r + 1) * blk, at * blk : (at + 1) * blk] = block


def total_kernel(bands, first, second):
    cores, half = 2, first.shape[1] // 2
    rows = first.shape[0]
    for c in range(cores):
        total = bands[c].astype(F32)
        for z in range(1, bands.shape[0] // cores):
            total += bands[z * cores + c].astype(F32)
        first[:, c * half : (c + 1) * half] = total[:, :half]
        second[c * rows : (c + 1) * rows, :] = total[:, half:]


def forward_kernel(
    odd,
    adj,
    adj_stale,
    feats,
    w_first,
    before_far,
    after_far,
    w_second_far,
    agg_t,
    hidden,
    slope,
    proj,
    within,
    across,
    stale_second,
    before,
    after,
    w_second,
    sems,
):
    pairs = [(before_far, before), (after_far, after), (w_second_far, w_second)]
    fetches = [pltpu.make_async_copy(src, dst, sems.at[i]) for i, (src, dst) in enumerate(pairs)]
    for fetch in fetches:
        fetch.start()
    hid = w_first.shape[1]
    step = min(256, hid)
    m = adj[...]
    agg = dot(m, feats[...], 1, 1).astype(BF)
    agg_t[...] = dot(feats[...], m, 1, 1).astype(BF)
    for fetch in fetches:
        fetch.wait()
    rows = before.shape[0]
    m_before, m_after = adj_stale[:, :rows], adj_stale[:, rows:]
    total = jnp.zeros(proj.shape, F32)
    for at in range(0, hid, step):
        cols = slice(at, at + step)
        a = dot(agg, w_first[:, cols], 1, 0)
        a += dot(m_before, before[:, cols], 1, 0) + dot(m_after, after[:, cols], 1, 0)
        s = jax.nn.sigmoid(a)
        h = (a * s).astype(BF)
        hidden[:, cols] = h
        slope[:, cols] = (s * (1.0 + a * (1.0 - s))).astype(BF)
        total += dot(h, w_second[cols, :], 1, 0)
    proj[...] = total.astype(BF)
    stale_second[...] = dot(m_before, before[:, hid:], 1, 0) + dot(m_after, after[:, hid:], 1, 0)
    blk = within.shape[0]
    top, bottom = proj[:blk], proj[proj.shape[0] - blk :]
    is_odd = odd[0] == 1
    within[...] = jnp.where(is_odd, top, bottom)
    across[...] = jnp.where(is_odd, bottom, top)


def middle_kernel(
    odd, adj, own, paired_in, crossed_in, stale, mark, logits, inner, within, across
):
    blk = within.shape[0]
    is_odd = odd[0] == 1
    up = jnp.where(is_odd, paired_in[...], crossed_in[...])
    down = jnp.where(is_odd, crossed_in[...], paired_in[...])
    size = own.shape[0]
    reach = size + 2 * blk
    agg = dot(adj[:, :blk], up, 1, 0)
    agg += dot(adj[:, blk : blk + size], own[...], 1, 0)
    agg += dot(adj[:, blk + size : reach], down, 1, 0)
    agg += stale[...]
    logits[...] = agg.astype(BF)
    e = jnp.exp(agg - jnp.max(agg, axis=1, keepdims=True))
    grad = (e / jnp.sum(e, axis=1, keepdims=True) - mark[...]).astype(BF)
    spread = dot(adj[:, :reach], grad, 0, 0)
    inner[...] = spread[blk : blk + size]
    rim_up, rim_down = spread[:blk], spread[blk + size :]
    within[...] = jnp.where(is_odd, rim_up, rim_down).astype(BF)
    across[...] = jnp.where(is_odd, rim_down, rim_up).astype(BF)


def backward_kernel(
    scale, odd, core, inner, paired_in, crossed_in, hidden, w_second, slope, agg_t, send, kept, grad_agg, second
):
    blk = paired_in.shape[0]
    size = inner.shape[0]
    hid = slope.shape[1]
    step = min(256, hid)
    half = hid // 2
    is_odd = odd[0] == 1
    mine, other = core[0], 1 - core[0]
    upper = inner[:blk] + jnp.where(is_odd, paired_in[...], crossed_in[...]).astype(F32)
    lower = inner[size - blk :] + jnp.where(is_odd, crossed_in[...], paired_in[...]).astype(F32)
    if size > 2 * blk:
        parts = [upper, inner[blk : size - blk], lower]
    else:
        parts = [upper, lower]
    grad_p2 = jnp.concatenate(parts, axis=0).astype(BF)
    for at in range(0, hid, step):
        cols = slice(at, at + step)
        grad_agg[:, cols] = (dot(grad_p2, w_second[cols, :], 1, 1) * slope[:, cols].astype(F32)).astype(BF)
    second[...] = (dot(hidden[...], grad_p2, 0, 0) * scale).reshape(second.shape)
    rows = second.shape[0] * second.shape[2]
    send[:, half:] = second[:, other].reshape(rows, second.shape[3]).astype(BF)
    kept[...] = second[:, mine].reshape(rows, second.shape[3])
    g = grad_agg[:, pl.ds(pl.multiple_of(other * half, half), half)]
    send[:, :half] = (dot(agg_t[...], g, 1, 0) * scale).astype(BF)


def feature_kernel(scale, core, grad_agg, adj, agg_t, kept, w_first_far, keep, out, w_first, sem):
    fetch = pltpu.make_async_copy(w_first_far, w_first, sem)
    fetch.start()
    width = out.shape[1]
    half = grad_agg.shape[1] // 2
    g = grad_agg[:, pl.ds(pl.multiple_of(core[0] * half, half), half)]
    keep[:, :half] = dot(agg_t[...], g, 1, 0) * scale
    keep[:, half:] = kept[...]
    fetch.wait()
    back = dot(w_first[...], grad_agg[...], 1, 1).astype(BF)
    out[...] = dot(back, adj[:, :width], 1, 0).astype(BF)


def whole_core(kernel, outs, blocks, scratch=(), flops=0, scalars=1, fetched=0):
    return pl.pallas_call(
        kernel,
        out_shape=[jax.ShapeDtypeStruct(*out) for out in outs],
        in_specs=[pl.BlockSpec(memory_space=pltpu.SMEM)] * scalars + [pl.BlockSpec(memory_space=pltpu.VMEM)] * blocks
        + [pl.BlockSpec(memory_space=pl.ANY)] * fetched,
        scratch_shapes=scratch,
        compiler_params=pltpu.CompilerParams(vmem_limit_bytes=16 * 1024 * 1024),
        cost_estimate=pl.CostEstimate(flops=flops, bytes_accessed=4_000_000, transcendentals=0),
    )


def local(feats_t, w_first, w_second, stale_rows, tile_vals, tile_src, tile_count, labels):
    blk = tile_vals.shape[-1]
    hid = w_first.shape[1]
    classes = w_second.shape[1]
    own = labels.shape[0]
    reach = own + 2 * blk
    n_grp, n_dom = lax.axis_size("grp"), lax.axis_size("dom")
    scale = 1.0 / math.sqrt(own * n_grp * n_dom)
    feat_rows = feats_t.shape[0]
    feat_all = feat_rows * n_dom
    half = hid // 2
    core = lax.axis_index("grp") % 2

    (wide,) = whole(widen_kernel, [((n_dom, feat_rows, reach), BF)])(feats_t)
    wide, tile_vals, stale_rows = lax.optimization_barrier((wide, tile_vals, stale_rows))
    feats = lax.all_to_all(wide, "dom", split_axis=0, concat_axis=0, tiled=True).reshape(feat_all, reach)

    adj, adj_stale = whole_core(adjacency_kernel, [((own, reach), BF), ((own, 2 * blk), BF)], 1, scalars=2)(
        tile_src, tile_count, tile_vals
    )
    stale_rows, adj, adj_stale = lax.optimization_barrier((stale_rows, adj, adj_stale))
    before = from_previous(stale_rows, "grp")
    after = from_next(stale_rows, "grp")
    mark = (labels[:, None] == jnp.arange(classes, dtype=jnp.int32)[None, :]).astype(F32)

    odd = (lax.axis_index("dom") % 2)[None]
    agg_t, hidden, slope, proj_second, within, across, stale_second = whole_core(
        forward_kernel,
        [
            ((feat_all, own), BF),
            ((own, hid), BF),
            ((own, hid), BF),
            ((own, classes), BF),
            ((blk, classes), BF),
            ((blk, classes), BF),
            ((own, classes), F32),
        ],
        4,
        scratch=[
            pltpu.VMEM(before.shape, BF),
            pltpu.VMEM(after.shape, BF),
            pltpu.VMEM(w_second.shape, BF),
            pltpu.SemaphoreType.DMA((3,)),
        ],
        fetched=3,
        flops=2 * own * (2 * feat_all * reach + feat_all * hid + hid * classes),
    )(odd, adj, adj_stale, feats, w_first, in_hbm(before), in_hbm(after), in_hbm(w_second))

    logits, inner, within, across = whole_core(
        middle_kernel,
        [((own, classes), BF), ((own, classes), F32), ((blk, classes), BF), ((blk, classes), BF)],
        6,
        flops=4 * own * reach * classes,
    )(
        odd,
        adj,
        proj_second,
        paired(within, "dom", 0),
        paired(across, "dom", 1),
        stale_second,
        mark,
    )

    width = half + classes
    send, kept, grad_agg = whole_core(
        functools.partial(backward_kernel, scale),
        [((feat_all, width), BF), ((feat_all, classes), F32), ((own, hid), BF)],
        7,
        scratch=[pltpu.VMEM((n_dom, 2, feat_rows, classes), F32)],
        flops=2 * own * (hid * classes * 2 + feat_all * half),
        scalars=2,
    )(odd, core[None], inner, paired(within, "dom", 0), paired(across, "dom", 1), hidden, w_second, slope, agg_t)
    received = swapped(send, "grp")

    keep, grad_wide = whole_core(
        functools.partial(feature_kernel, scale),
        [((feat_all, width), F32), ((feat_all, reach), BF)],
        4,
        scratch=[pltpu.VMEM((feat_all, hid), BF), pltpu.SemaphoreType.DMA],
        fetched=1,
        flops=2 * own * (hid * feat_all + reach * feat_all + feat_all * half),
    )(core[None], grad_agg, adj, agg_t, kept, in_hbm(w_first))
    summed = (keep + received.astype(F32)).astype(BF)
    sent = jnp.concatenate([summed, grad_wide], axis=1)
    got = lax.all_to_all(sent, "dom", split_axis=0, concat_axis=0, tiled=True).reshape(n_dom, feat_rows, -1)

    band = jnp.sum(got[:, :, :width].astype(F32), axis=0).astype(BF)
    copies = jnp.broadcast_to(band[None], (n_grp, feat_rows, width))
    bands = lax.all_to_all(copies, "grp", split_axis=0, concat_axis=0, tiled=True)
    grad_first, grad_second = whole(
        total_kernel, [((feat_rows, hid), F32), ((2 * feat_rows, classes), F32)]
    )(bands)

    wide_back = got[:, :, width:].astype(F32)
    none = jnp.zeros((1, feat_rows, blk), F32)
    first_block = jnp.concatenate([none, wide_back[:-1, :, reach - blk :]], axis=0)
    last_block = jnp.concatenate([wide_back[1:, :, :blk], none], axis=0)
    middle = jnp.zeros((n_dom, feat_rows, own - blk), F32)
    grad_feats = (
        wide_back[:, :, blk : reach - blk]
        + jnp.concatenate([first_block, middle], axis=2)
        + jnp.concatenate([middle, last_block], axis=2)
    )
    grad_feats = grad_feats.astype(BF).transpose(1, 0, 2).reshape(feat_rows, n_dom * own)
    return (logits, grad_feats, grad_first, grad_second)


def solution(mesh):
    return jax.shard_map(
        local,
        mesh=mesh,
        in_specs=(
            P("dom", "grp"),
            P(),
            P(),
            P(("grp", "dom"), None),
            P(("grp", "dom"), None, None, None),
            P(("grp", "dom"), None),
            P(("grp", "dom")),
            P(("grp", "dom")),
        ),
        out_specs=(P(("grp", "dom"), None), P("dom", "grp"), P("dom", None), P("dom", None)),
        check_vma=False,
    )
```

```python
import functools
import math

import jax
import jax.numpy as jnp
from jax import lax
from jax.experimental import pallas as pl
from jax.experimental.pallas import tpu as pltpu
from jax.sharding import PartitionSpec as P

BF = jnp.bfloat16
F32 = jnp.float32


def dot(a, b, ca, cb):
    return lax.dot_general(a, b, (((ca,), (cb,)), ((), ())), preferred_element_type=F32)


def swapped(x, axis):
    count = lax.axis_size(axis)
    return lax.ppermute(x, axis, [(i, i ^ 1) for i in range(count)])


def from_previous(x, axis):
    count = lax.axis_size(axis)
    return lax.ppermute(x, axis, [(i, i + 1) for i in range(count - 1)])


def from_next(x, axis):
    count = lax.axis_size(axis)
    return lax.ppermute(x, axis, [(i + 1, i) for i in range(count - 1)])


def paired(x, axis, first):
    count = lax.axis_size(axis)
    pairs = []
    for i in range(first, count - 1, 2):
        pairs += [(i, i + 1), (i + 1, i)]
    return lax.ppermute(x, axis, pairs)


def in_hbm(x):
    return pltpu.with_memory_space_constraint(x, pltpu.HBM)


def whole(kernel, outs, scratch=(), flops=0):
    return pl.pallas_call(
        kernel,
        out_shape=[jax.ShapeDtypeStruct(*out) for out in outs],
        scratch_shapes=list(scratch),
        compiler_params=pltpu.CompilerParams(vmem_limit_bytes=16 * 1024 * 1024),
        cost_estimate=pl.CostEstimate(flops=flops, bytes_accessed=4_000_000, transcendentals=0),
    )


def widen_kernel(feats, wide):
    parts, rows, reach = wide.shape
    own = feats.shape[1] // parts
    blk = (reach - own) // 2
    none = jnp.zeros((rows, blk), wide.dtype)
    for d in range(parts):
        first, last = d * own - blk, (d + 1) * own + blk
        wide[d, :, blk : blk + own] = feats[:, d * own : (d + 1) * own]
        wide[d, :, :blk] = feats[:, first : first + blk] if d > 0 else none
        wide[d, :, blk + own :] = feats[:, last - blk : last] if d < parts - 1 else none


def adjacency_kernel(src, count, tiles, adj, adj_stale):
    block_rows, slots, blk, _ = tiles.shape
    for r in range(block_rows):
        live = count[r]
        inside = adj.shape[1] // blk
        for t in range(inside + adj_stale.shape[1] // blk):
            block = jnp.zeros((blk, blk), BF)
            for k in range(slots):
                hit = jnp.logical_and(src[r, k] == t, k < live)
                block = jnp.where(hit, tiles[r, k], block)
            out, at = (adj, t) if t < inside else (adj_stale, t - inside)
            out[r * blk : (r + 1) * blk, at * blk : (at + 1) * blk] = block


def total_kernel(bands, first, second):
    cores, half = 2, first.shape[1] // 2
    rows = first.shape[0]
    for c in range(cores):
        total = bands[c].astype(F32)
        for z in range(1, bands.shape[0] // cores):
            total += bands[z * cores + c].astype(F32)
        first[:, c * half : (c + 1) * half] = total[:, :half]
        second[c * rows : (c + 1) * rows, :] = total[:, half:]


def stale_kernel(adj_stale, before, after, first, second, rows, sems):
    count = before.shape[0]
    fetches = [
        pltpu.make_async_copy(before, rows.at[:count], sems.at[0]),
        pltpu.make_async_copy(after, rows.at[count:], sems.at[1]),
    ]
    for fetch in fetches:
        fetch.start()
    for fetch in fetches:
        fetch.wait()
    hid = first.shape[1]
    first[...] = dot(adj_stale[...], rows[:, :hid], 1, 0)
    second[...] = dot(adj_stale[...], rows[:, hid:], 1, 0)


def forward_kernel(
    odd, adj, feats, stale, w_second, w_first_far, agg_t, hidden, slope, proj, within, across, w_first, sems
):
    hid = w_first.shape[1]
    step = hid // sems.shape[0]
    fetches = []
    for i in range(sems.shape[0]):
        cols = slice(i * step, (i + 1) * step)
        fetches.append(pltpu.make_async_copy(w_first_far.at[:, cols], w_first.at[:, cols], sems.at[i]))
    for fetch in fetches:
        fetch.start()
    m = adj[...]
    agg = dot(m, feats[...], 1, 1).astype(BF)
    agg_t[...] = dot(feats[...], m, 1, 1).astype(BF)
    total = jnp.zeros(proj.shape, F32)
    for at in range(0, hid, step):
        cols = slice(at, at + step)
        fetches[at // step].wait()
        a = dot(agg, w_first[:, cols], 1, 0) + stale[:, cols]
        s = jax.nn.sigmoid(a)
        h = (a * s).astype(BF)
        hidden[:, cols] = h
        slope[:, cols] = (s * (1.0 + a * (1.0 - s))).astype(BF)
        total += dot(h, w_second[cols, :], 1, 0)
    proj[...] = total.astype(BF)
    blk = within.shape[0]
    top, bottom = proj[:blk], proj[proj.shape[0] - blk :]
    is_odd = odd[0] == 1
    within[...] = jnp.where(is_odd, top, bottom)
    across[...] = jnp.where(is_odd, bottom, top)


def middle_kernel(
    odd, adj, own, paired_in, crossed_in, stale, mark, logits, inner, within, across
):
    blk = within.shape[0]
    is_odd = odd[0] == 1
    up = jnp.where(is_odd, paired_in[...], crossed_in[...])
    down = jnp.where(is_odd, crossed_in[...], paired_in[...])
    size = own.shape[0]
    reach = size + 2 * blk
    agg = dot(adj[:, :blk], up, 1, 0)
    agg += dot(adj[:, blk : blk + size], own[...], 1, 0)
    agg += dot(adj[:, blk + size : reach], down, 1, 0)
    agg += stale[...]
    logits[...] = agg.astype(BF)
    e = jnp.exp(agg - jnp.max(agg, axis=1, keepdims=True))
    grad = (e / jnp.sum(e, axis=1, keepdims=True) - mark[...]).astype(BF)
    spread = dot(adj[:, :reach], grad, 0, 0)
    inner[...] = spread[blk : blk + size]
    rim_up, rim_down = spread[:blk], spread[blk + size :]
    within[...] = jnp.where(is_odd, rim_up, rim_down).astype(BF)
    across[...] = jnp.where(is_odd, rim_down, rim_up).astype(BF)


def backward_kernel(
    scale, odd, core, inner, paired_in, crossed_in, hidden, w_second, slope, agg_t, send, kept, grad_agg, second
):
    blk = paired_in.shape[0]
    size = inner.shape[0]
    hid = slope.shape[1]
    step = min(256, hid)
    half = hid // 2
    is_odd = odd[0] == 1
    mine, other = core[0], 1 - core[0]
    upper = inner[:blk] + jnp.where(is_odd, paired_in[...], crossed_in[...]).astype(F32)
    lower = inner[size - blk :] + jnp.where(is_odd, crossed_in[...], paired_in[...]).astype(F32)
    if size > 2 * blk:
        parts = [upper, inner[blk : size - blk], lower]
    else:
        parts = [upper, lower]
    grad_p2 = jnp.concatenate(parts, axis=0).astype(BF)
    for at in range(0, hid, step):
        cols = slice(at, at + step)
        grad_agg[:, cols] = (dot(grad_p2, w_second[cols, :], 1, 1) * slope[:, cols].astype(F32)).astype(BF)
    second[...] = (dot(hidden[...], grad_p2, 0, 0) * scale).reshape(second.shape)
    rows = second.shape[0] * second.shape[2]
    send[:, half:] = second[:, other].reshape(rows, second.shape[3]).astype(BF)
    kept[...] = second[:, mine].reshape(rows, second.shape[3])
    g = grad_agg[:, pl.ds(pl.multiple_of(other * half, half), half)]
    send[:, :half] = (dot(agg_t[...], g, 1, 0) * scale).astype(BF)


def feature_kernel(scale, core, grad_agg, adj, agg_t, kept, w_first_far, keep, out, w_first, sem):
    fetch = pltpu.make_async_copy(w_first_far, w_first, sem)
    fetch.start()
    width = out.shape[1]
    half = grad_agg.shape[1] // 2
    g = grad_agg[:, pl.ds(pl.multiple_of(core[0] * half, half), half)]
    keep[:, :half] = dot(agg_t[...], g, 1, 0) * scale
    keep[:, half:] = kept[...]
    fetch.wait()
    back = dot(w_first[...], grad_agg[...], 1, 1).astype(BF)
    out[...] = dot(back, adj[:, :width], 1, 0).astype(BF)


def whole_core(kernel, outs, blocks, scratch=(), flops=0, scalars=1, fetched=0):
    return pl.pallas_call(
        kernel,
        out_shape=[jax.ShapeDtypeStruct(*out) for out in outs],
        in_specs=[pl.BlockSpec(memory_space=pltpu.SMEM)] * scalars + [pl.BlockSpec(memory_space=pltpu.VMEM)] * blocks
        + [pl.BlockSpec(memory_space=pl.ANY)] * fetched,
        scratch_shapes=scratch,
        compiler_params=pltpu.CompilerParams(vmem_limit_bytes=16 * 1024 * 1024),
        cost_estimate=pl.CostEstimate(flops=flops, bytes_accessed=4_000_000, transcendentals=0),
    )


def local(feats_t, w_first, w_second, stale_rows, tile_vals, tile_src, tile_count, labels):
    blk = tile_vals.shape[-1]
    hid = w_first.shape[1]
    classes = w_second.shape[1]
    own = labels.shape[0]
    reach = own + 2 * blk
    n_grp, n_dom = lax.axis_size("grp"), lax.axis_size("dom")
    scale = 1.0 / math.sqrt(own * n_grp * n_dom)
    feat_rows = feats_t.shape[0]
    feat_all = feat_rows * n_dom
    half = hid // 2
    core = lax.axis_index("grp") % 2

    (wide,) = whole(widen_kernel, [((n_dom, feat_rows, reach), BF)])(feats_t)
    wide, tile_vals, stale_rows = lax.optimization_barrier((wide, tile_vals, stale_rows))
    feats = lax.all_to_all(wide, "dom", split_axis=0, concat_axis=0, tiled=True).reshape(feat_all, reach)

    adj, adj_stale = whole_core(adjacency_kernel, [((own, reach), BF), ((own, 2 * blk), BF)], 1, scalars=2)(
        tile_src, tile_count, tile_vals
    )
    stale_rows, adj, adj_stale = lax.optimization_barrier((stale_rows, adj, adj_stale))
    before = from_previous(stale_rows, "grp")
    after = from_next(stale_rows, "grp")
    stale_first, stale_second = whole_core(
        stale_kernel,
        [((own, hid), F32), ((own, classes), F32)],
        1,
        scratch=[pltpu.VMEM((2 * blk, hid + classes), BF), pltpu.SemaphoreType.DMA((2,))],
        flops=2 * own * 2 * blk * (hid + classes),
        scalars=0,
        fetched=2,
    )(adj_stale, in_hbm(before), in_hbm(after))
    mark = (labels[:, None] == jnp.arange(classes, dtype=jnp.int32)[None, :]).astype(F32)

    odd = ((lax.axis_index("dom") + 1) % 2)[None]
    agg_t, hidden, slope, proj_second, within, across = whole_core(
        forward_kernel,
        [
            ((feat_all, own), BF),
            ((own, hid), BF),
            ((own, hid), BF),
            ((own, classes), BF),
            ((blk, classes), BF),
            ((blk, classes), BF),
        ],
        4,
        scratch=[pltpu.VMEM((feat_all, hid), BF), pltpu.SemaphoreType.DMA((4,))],
        fetched=1,
        flops=2 * own * (2 * feat_all * reach + feat_all * hid + hid * classes),
    )(odd, adj, feats, stale_first, w_second, in_hbm(w_first))

    logits, inner, within, across = whole_core(
        middle_kernel,
        [((own, classes), BF), ((own, classes), F32), ((blk, classes), BF), ((blk, classes), BF)],
        6,
        flops=4 * own * reach * classes,
    )(
        odd,
        adj,
        proj_second,
        paired(within, "dom", 1),
        paired(across, "dom", 0),
        stale_second,
        mark,
    )

    width = half + classes
    send, kept, grad_agg = whole_core(
        functools.partial(backward_kernel, scale),
        [((feat_all, width), BF), ((feat_all, classes), F32), ((own, hid), BF)],
        7,
        scratch=[pltpu.VMEM((n_dom, 2, feat_rows, classes), F32)],
        flops=2 * own * (hid * classes * 2 + feat_all * half),
        scalars=2,
    )(odd, core[None], inner, paired(within, "dom", 1), paired(across, "dom", 0), hidden, w_second, slope, agg_t)
    received = swapped(send, "grp")

    keep, grad_wide = whole_core(
        functools.partial(feature_kernel, scale),
        [((feat_all, width), F32), ((feat_all, reach), BF)],
        4,
        scratch=[pltpu.VMEM((feat_all, hid), BF), pltpu.SemaphoreType.DMA],
        fetched=1,
        flops=2 * own * (hid * feat_all + reach * feat_all + feat_all * half),
    )(core[None], grad_agg, adj, agg_t, kept, in_hbm(w_first))
    summed = (keep + received.astype(F32)).astype(BF)
    sent = jnp.concatenate([summed, grad_wide], axis=1)
    got = lax.all_to_all(sent, "dom", split_axis=0, concat_axis=0, tiled=True).reshape(n_dom, feat_rows, -1)

    band = jnp.sum(got[:, :, :width].astype(F32), axis=0).astype(BF)
    copies = jnp.broadcast_to(band[None], (n_grp, feat_rows, width))
    bands = lax.all_to_all(copies, "grp", split_axis=0, concat_axis=0, tiled=True)
    grad_first, grad_second = whole(
        total_kernel, [((feat_rows, hid), F32), ((2 * feat_rows, classes), F32)]
    )(bands)

    wide_back = got[:, :, width:].astype(F32)
    none = jnp.zeros((1, feat_rows, blk), F32)
    first_block = jnp.concatenate([none, wide_back[:-1, :, reach - blk :]], axis=0)
    last_block = jnp.concatenate([wide_back[1:, :, :blk], none], axis=0)
    middle = jnp.zeros((n_dom, feat_rows, own - blk), F32)
    grad_feats = (
        wide_back[:, :, blk : reach - blk]
        + jnp.concatenate([first_block, middle], axis=2)
        + jnp.concatenate([middle, last_block], axis=2)
    )
    grad_feats = grad_feats.astype(BF).transpose(1, 0, 2).reshape(feat_rows, n_dom * own)
    return (logits, grad_feats, grad_first, grad_second)


def solution(mesh):
    return jax.shard_map(
        local,
        mesh=mesh,
        in_specs=(
            P("dom", "grp"),
            P(),
            P(),
            P(("grp", "dom"), None),
            P(("grp", "dom"), None, None, None),
            P(("grp", "dom"), None),
            P(("grp", "dom")),
            P(("grp", "dom")),
        ),
        out_specs=(P(("grp", "dom"), None), P("dom", "grp"), P("dom", None), P("dom", None)),
        check_vma=False,
    )
```

```python
import functools
import math

import jax
import jax.numpy as jnp
from jax import lax
from jax.experimental import pallas as pl
from jax.experimental.pallas import tpu as pltpu
from jax.sharding import PartitionSpec as P

BF = jnp.bfloat16
F32 = jnp.float32


def dot(a, b, ca, cb):
    return lax.dot_general(a, b, (((ca,), (cb,)), ((), ())), preferred_element_type=F32)


def swapped(x, axis):
    count = lax.axis_size(axis)
    return lax.ppermute(x, axis, [(i, i ^ 1) for i in range(count)])


def from_previous(x, axis):
    count = lax.axis_size(axis)
    return lax.ppermute(x, axis, [(i, i + 1) for i in range(count - 1)])


def from_next(x, axis):
    count = lax.axis_size(axis)
    return lax.ppermute(x, axis, [(i + 1, i) for i in range(count - 1)])


def paired(x, axis, first):
    count = lax.axis_size(axis)
    pairs = []
    for i in range(first, count - 1, 2):
        pairs += [(i, i + 1), (i + 1, i)]
    return lax.ppermute(x, axis, pairs)


def in_hbm(x):
    return pltpu.with_memory_space_constraint(x, pltpu.HBM)


def whole(kernel, outs, scratch=(), flops=0):
    return pl.pallas_call(
        kernel,
        out_shape=[jax.ShapeDtypeStruct(*out) for out in outs],
        scratch_shapes=list(scratch),
        compiler_params=pltpu.CompilerParams(vmem_limit_bytes=16 * 1024 * 1024),
        cost_estimate=pl.CostEstimate(flops=flops, bytes_accessed=4_000_000, transcendentals=0),
    )


def widen_kernel(feats, wide):
    parts, rows, reach = wide.shape
    own = feats.shape[1] // parts
    blk = (reach - own) // 2
    none = jnp.zeros((rows, blk), wide.dtype)
    for d in range(parts):
        first, last = d * own - blk, (d + 1) * own + blk
        wide[d, :, blk : blk + own] = feats[:, d * own : (d + 1) * own]
        wide[d, :, :blk] = feats[:, first : first + blk] if d > 0 else none
        wide[d, :, blk + own :] = feats[:, last - blk : last] if d < parts - 1 else none


def adjacency_kernel(src, count, tiles, adj, adj_stale):
    block_rows, slots, blk, _ = tiles.shape
    for r in range(block_rows):
        live = count[r]
        inside = adj.shape[1] // blk
        for t in range(inside + adj_stale.shape[1] // blk):
            block = jnp.zeros((blk, blk), BF)
            for k in range(slots):
                hit = jnp.logical_and(src[r, k] == t, k < live)
                block = jnp.where(hit, tiles[r, k], block)
            out, at = (adj, t) if t < inside else (adj_stale, t - inside)
            out[r * blk : (r + 1) * blk, at * blk : (at + 1) * blk] = block


def total_kernel(bands, first, second):
    cores, half = 2, first.shape[1] // 2
    rows = first.shape[0]
    for c in range(cores):
        total = bands[c].astype(F32)
        for z in range(1, bands.shape[0] // cores):
            total += bands[z * cores + c].astype(F32)
        first[:, c * half : (c + 1) * half] = total[:, :half]
        second[c * rows : (c + 1) * rows, :] = total[:, half:]


def stale_kernel(adj_stale, before, after, first, second, rows, sems):
    count = before.shape[0]
    fetches = [
        pltpu.make_async_copy(before, rows.at[:count], sems.at[0]),
        pltpu.make_async_copy(after, rows.at[count:], sems.at[1]),
    ]
    for fetch in fetches:
        fetch.start()
    for fetch in fetches:
        fetch.wait()
    hid = first.shape[1]
    first[...] = dot(adj_stale[...], rows[:, :hid], 1, 0).astype(BF)
    second[...] = dot(adj_stale[...], rows[:, hid:], 1, 0)


def forward_kernel(
    odd, adj, feats, w_first, stale, w_second_far, hidden, slope, proj, within, across, w_second, sem
):
    fetch = pltpu.make_async_copy(w_second_far, w_second, sem)
    fetch.start()
    hid = w_first.shape[1]
    step = min(256, hid)
    agg = dot(adj[...], feats[...], 1, 1).astype(BF)
    for at in range(0, hid, step):
        cols = slice(at, at + step)
        a = dot(agg, w_first[:, cols], 1, 0) + stale[:, cols].astype(F32)
        s = jax.nn.sigmoid(a)
        hidden[:, cols] = (a * s).astype(BF)
        slope[:, cols] = (s * (1.0 + a * (1.0 - s))).astype(BF)
    fetch.wait()
    proj[...] = dot(hidden[...], w_second[...], 1, 0).astype(BF)
    blk = within.shape[0]
    top, bottom = proj[:blk], proj[proj.shape[0] - blk :]
    is_odd = odd[0] == 1
    within[...] = jnp.where(is_odd, top, bottom)
    across[...] = jnp.where(is_odd, bottom, top)


def aggregate_kernel(feats, adj, agg_t):
    agg_t[...] = dot(feats[...], adj[...], 1, 1).astype(BF)


def middle_kernel(
    odd, adj, own, paired_in, crossed_in, stale, mark, logits, inner, within, across
):
    blk = within.shape[0]
    is_odd = odd[0] == 1
    up = jnp.where(is_odd, paired_in[...], crossed_in[...])
    down = jnp.where(is_odd, crossed_in[...], paired_in[...])
    size = own.shape[0]
    reach = size + 2 * blk
    agg = dot(adj[:, :blk], up, 1, 0)
    agg += dot(adj[:, blk : blk + size], own[...], 1, 0)
    agg += dot(adj[:, blk + size : reach], down, 1, 0)
    agg += stale[...]
    logits[...] = agg.astype(BF)
    e = jnp.exp(agg - jnp.max(agg, axis=1, keepdims=True))
    grad = (e / jnp.sum(e, axis=1, keepdims=True) - mark[...]).astype(BF)
    spread = dot(adj[:, :reach], grad, 0, 0)
    inner[...] = spread[blk : blk + size]
    rim_up, rim_down = spread[:blk], spread[blk + size :]
    within[...] = jnp.where(is_odd, rim_up, rim_down).astype(BF)
    across[...] = jnp.where(is_odd, rim_down, rim_up).astype(BF)


def backward_kernel(
    scale, odd, core, inner, paired_in, crossed_in, hidden, w_second, slope, agg_t, send, kept, grad_agg, second
):
    blk = paired_in.shape[0]
    size = inner.shape[0]
    hid = slope.shape[1]
    step = min(256, hid)
    half = hid // 2
    is_odd = odd[0] == 1
    mine, other = core[0], 1 - core[0]
    upper = inner[:blk] + jnp.where(is_odd, paired_in[...], crossed_in[...]).astype(F32)
    lower = inner[size - blk :] + jnp.where(is_odd, crossed_in[...], paired_in[...]).astype(F32)
    if size > 2 * blk:
        parts = [upper, inner[blk : size - blk], lower]
    else:
        parts = [upper, lower]
    grad_p2 = jnp.concatenate(parts, axis=0).astype(BF)
    for at in range(0, hid, step):
        cols = slice(at, at + step)
        grad_agg[:, cols] = (dot(grad_p2, w_second[cols, :], 1, 1) * slope[:, cols].astype(F32)).astype(BF)
    second[...] = (dot(hidden[...], grad_p2, 0, 0) * scale).reshape(second.shape)
    rows = second.shape[0] * second.shape[2]
    send[:, half:] = second[:, other].reshape(rows, second.shape[3]).astype(BF)
    kept[...] = second[:, mine].reshape(rows, second.shape[3])
    g = grad_agg[:, pl.ds(pl.multiple_of(other * half, half), half)]
    send[:, :half] = (dot(agg_t[...], g, 1, 0) * scale).astype(BF)


def feature_kernel(scale, core, grad_agg, adj, agg_t, kept, w_first_far, keep, out, w_first, sem):
    fetch = pltpu.make_async_copy(w_first_far, w_first, sem)
    fetch.start()
    width = out.shape[1]
    half = grad_agg.shape[1] // 2
    g = grad_agg[:, pl.ds(pl.multiple_of(core[0] * half, half), half)]
    keep[:, :half] = dot(agg_t[...], g, 1, 0) * scale
    keep[:, half:] = kept[...]
    fetch.wait()
    back = dot(w_first[...], grad_agg[...], 1, 1).astype(BF)
    out[...] = dot(back, adj[:, :width], 1, 0).astype(BF)


def whole_core(kernel, outs, blocks, scratch=(), flops=0, scalars=1, fetched=0):
    return pl.pallas_call(
        kernel,
        out_shape=[jax.ShapeDtypeStruct(*out) for out in outs],
        in_specs=[pl.BlockSpec(memory_space=pltpu.SMEM)] * scalars + [pl.BlockSpec(memory_space=pltpu.VMEM)] * blocks
        + [pl.BlockSpec(memory_space=pl.ANY)] * fetched,
        scratch_shapes=scratch,
        compiler_params=pltpu.CompilerParams(vmem_limit_bytes=16 * 1024 * 1024),
        cost_estimate=pl.CostEstimate(flops=flops, bytes_accessed=4_000_000, transcendentals=0),
    )


def local(feats_t, w_first, w_second, stale_rows, tile_vals, tile_src, tile_count, labels):
    blk = tile_vals.shape[-1]
    hid = w_first.shape[1]
    classes = w_second.shape[1]
    own = labels.shape[0]
    reach = own + 2 * blk
    n_grp, n_dom = lax.axis_size("grp"), lax.axis_size("dom")
    scale = 1.0 / math.sqrt(own * n_grp * n_dom)
    feat_rows = feats_t.shape[0]
    feat_all = feat_rows * n_dom
    half = hid // 2
    core = lax.axis_index("grp") % 2

    (wide,) = whole(widen_kernel, [((n_dom, feat_rows, reach), BF)])(feats_t)
    wide, tile_vals, stale_rows = lax.optimization_barrier((wide, tile_vals, stale_rows))
    feats = lax.all_to_all(wide, "dom", split_axis=0, concat_axis=0, tiled=True).reshape(feat_all, reach)

    adj, adj_stale = whole_core(adjacency_kernel, [((own, reach), BF), ((own, 2 * blk), BF)], 1, scalars=2)(
        tile_src, tile_count, tile_vals
    )
    stale_rows, adj, adj_stale = lax.optimization_barrier((stale_rows, adj, adj_stale))
    before = from_previous(stale_rows, "grp")
    after = from_next(stale_rows, "grp")
    stale_first, stale_second = whole_core(
        stale_kernel,
        [((own, hid), BF), ((own, classes), F32)],
        1,
        scratch=[pltpu.VMEM((2 * blk, hid + classes), BF), pltpu.SemaphoreType.DMA((2,))],
        flops=2 * own * 2 * blk * (hid + classes),
        scalars=0,
        fetched=2,
    )(adj_stale, in_hbm(before), in_hbm(after))
    mark = (labels[:, None] == jnp.arange(classes, dtype=jnp.int32)[None, :]).astype(F32)

    odd = ((lax.axis_index("dom") + 1) % 2)[None]
    hidden, slope, proj_second, within, across = whole_core(
        forward_kernel,
        [
            ((own, hid), BF),
            ((own, hid), BF),
            ((own, classes), BF),
            ((blk, classes), BF),
            ((blk, classes), BF),
        ],
        4,
        scratch=[pltpu.VMEM((hid, classes), BF), pltpu.SemaphoreType.DMA],
        fetched=1,
        flops=2 * own * (feat_all * reach + feat_all * hid + hid * classes),
    )(odd, adj, feats, w_first, stale_first, in_hbm(w_second))
    feats, adj_beside, within = lax.optimization_barrier((feats, adj, within))
    (agg_t,) = whole(aggregate_kernel, [((feat_all, own), BF)], flops=2 * own * feat_all * reach)(feats, adj_beside)

    logits, inner, within, across = whole_core(
        middle_kernel,
        [((own, classes), BF), ((own, classes), F32), ((blk, classes), BF), ((blk, classes), BF)],
        6,
        flops=4 * own * reach * classes,
    )(
        odd,
        adj,
        proj_second,
        paired(within, "dom", 1),
        paired(across, "dom", 0),
        stale_second,
        mark,
    )

    width = half + classes
    send, kept, grad_agg = whole_core(
        functools.partial(backward_kernel, scale),
        [((feat_all, width), BF), ((feat_all, classes), F32), ((own, hid), BF)],
        7,
        scratch=[pltpu.VMEM((n_dom, 2, feat_rows, classes), F32)],
        flops=2 * own * (hid * classes * 2 + feat_all * half),
        scalars=2,
    )(odd, core[None], inner, paired(within, "dom", 1), paired(across, "dom", 0), hidden, w_second, slope, agg_t)
    received = swapped(send, "grp")

    keep, grad_wide = whole_core(
        functools.partial(feature_kernel, scale),
        [((feat_all, width), F32), ((feat_all, reach), BF)],
        4,
        scratch=[pltpu.VMEM((feat_all, hid), BF), pltpu.SemaphoreType.DMA],
        fetched=1,
        flops=2 * own * (hid * feat_all + reach * feat_all + feat_all * half),
    )(core[None], grad_agg, adj, agg_t, kept, in_hbm(w_first))
    summed = (keep + received.astype(F32)).astype(BF)
    sent = jnp.concatenate([summed, grad_wide], axis=1)
    got = lax.all_to_all(sent, "dom", split_axis=0, concat_axis=0, tiled=True).reshape(n_dom, feat_rows, -1)

    band = jnp.sum(got[:, :, :width].astype(F32), axis=0).astype(BF)
    copies = jnp.broadcast_to(band[None], (n_grp, feat_rows, width))
    bands = lax.all_to_all(copies, "grp", split_axis=0, concat_axis=0, tiled=True)
    grad_first, grad_second = whole(
        total_kernel, [((feat_rows, hid), F32), ((2 * feat_rows, classes), F32)]
    )(bands)

    wide_back = got[:, :, width:].astype(F32)
    none = jnp.zeros((1, feat_rows, blk), F32)
    first_block = jnp.concatenate([none, wide_back[:-1, :, reach - blk :]], axis=0)
    last_block = jnp.concatenate([wide_back[1:, :, :blk], none], axis=0)
    middle = jnp.zeros((n_dom, feat_rows, own - blk), F32)
    grad_feats = (
        wide_back[:, :, blk : reach - blk]
        + jnp.concatenate([first_block, middle], axis=2)
        + jnp.concatenate([middle, last_block], axis=2)
    )
    grad_feats = grad_feats.astype(BF).transpose(1, 0, 2).reshape(feat_rows, n_dom * own)
    return (logits, grad_feats, grad_first, grad_second)


def solution(mesh):
    return jax.shard_map(
        local,
        mesh=mesh,
        in_specs=(
            P("dom", "grp"),
            P(),
            P(),
            P(("grp", "dom"), None),
            P(("grp", "dom"), None, None, None),
            P(("grp", "dom"), None),
            P(("grp", "dom")),
            P(("grp", "dom")),
        ),
        out_specs=(P(("grp", "dom"), None), P("dom", "grp"), P("dom", None), P("dom", None)),
        check_vma=False,
    )
```

```python
import functools
import math

import jax
import jax.numpy as jnp
from jax import lax
from jax.experimental import pallas as pl
from jax.experimental.pallas import tpu as pltpu
from jax.sharding import PartitionSpec as P

BF = jnp.bfloat16
F32 = jnp.float32


def dot(a, b, ca, cb):
    return lax.dot_general(a, b, (((ca,), (cb,)), ((), ())), preferred_element_type=F32)


def swapped(x, axis):
    count = lax.axis_size(axis)
    return lax.ppermute(x, axis, [(i, i ^ 1) for i in range(count)])


def from_previous(x, axis):
    count = lax.axis_size(axis)
    return lax.ppermute(x, axis, [(i, i + 1) for i in range(count - 1)])


def from_next(x, axis):
    count = lax.axis_size(axis)
    return lax.ppermute(x, axis, [(i + 1, i) for i in range(count - 1)])


def paired(x, axis, first):
    count = lax.axis_size(axis)
    pairs = []
    for i in range(first, count - 1, 2):
        pairs += [(i, i + 1), (i + 1, i)]
    return lax.ppermute(x, axis, pairs)


def in_hbm(x):
    return pltpu.with_memory_space_constraint(x, pltpu.HBM)


def whole(kernel, outs, scratch=(), flops=0):
    return pl.pallas_call(
        kernel,
        out_shape=[jax.ShapeDtypeStruct(*out) for out in outs],
        scratch_shapes=list(scratch),
        compiler_params=pltpu.CompilerParams(vmem_limit_bytes=16 * 1024 * 1024),
        cost_estimate=pl.CostEstimate(flops=flops, bytes_accessed=4_000_000, transcendentals=0),
    )


def widen_kernel(feats, wide):
    parts, rows, reach = wide.shape
    own = feats.shape[1] // parts
    blk = (reach - own) // 2
    none = jnp.zeros((rows, blk), wide.dtype)
    for d in range(parts):
        first, last = d * own - blk, (d + 1) * own + blk
        wide[d, :, blk : blk + own] = feats[:, d * own : (d + 1) * own]
        wide[d, :, :blk] = feats[:, first : first + blk] if d > 0 else none
        wide[d, :, blk + own :] = feats[:, last - blk : last] if d < parts - 1 else none


def adjacency_kernel(src, count, tiles, adj, adj_stale):
    block_rows, slots, blk, _ = tiles.shape
    for r in range(block_rows):
        live = count[r]
        inside = adj.shape[1] // blk
        for t in range(inside + adj_stale.shape[1] // blk):
            block = jnp.zeros((blk, blk), BF)
            for k in range(slots):
                hit = jnp.logical_and(src[r, k] == t, k < live)
                block = jnp.where(hit, tiles[r, k], block)
            out, at = (adj, t) if t < inside else (adj_stale, t - inside)
            out[r * blk : (r + 1) * blk, at * blk : (at + 1) * blk] = block


def total_kernel(bands, first, second):
    cores, half = 2, first.shape[1] // 2
    rows = first.shape[0]
    for c in range(cores):
        total = bands[c].astype(F32)
        for z in range(1, bands.shape[0] // cores):
            total += bands[z * cores + c].astype(F32)
        first[:, c * half : (c + 1) * half] = total[:, :half]
        second[c * rows : (c + 1) * rows, :] = total[:, half:]


def stale_kernel(adj_stale, before, after, first, second, rows):
    count = before.shape[0]
    rows[:count] = before[...]
    rows[count:] = after[...]
    hid = first.shape[1]
    first[...] = dot(adj_stale[...], rows[:, :hid], 1, 0).astype(BF)
    second[...] = dot(adj_stale[...], rows[:, hid:], 1, 0)


def forward_kernel(
    odd, adj, feats, w_first, stale, w_second_far, hidden, slope, proj, within, across, w_second, sem
):
    fetch = pltpu.make_async_copy(w_second_far, w_second, sem)
    fetch.start()
    hid = w_first.shape[1]
    step = min(256, hid)
    agg = dot(adj[...], feats[...], 1, 1).astype(BF)
    for at in range(0, hid, step):
        cols = slice(at, at + step)
        a = dot(agg, w_first[:, cols], 1, 0) + stale[:, cols].astype(F32)
        s = jax.nn.sigmoid(a)
        hidden[:, cols] = (a * s).astype(BF)
        slope[:, cols] = (s * (1.0 + a * (1.0 - s))).astype(BF)
    fetch.wait()
    proj[...] = dot(hidden[...], w_second[...], 1, 0).astype(BF)
    blk = within.shape[0]
    top, bottom = proj[:blk], proj[proj.shape[0] - blk :]
    is_odd = odd[0] == 1
    within[...] = jnp.where(is_odd, top, bottom)
    across[...] = jnp.where(is_odd, bottom, top)


def aggregate_kernel(feats, adj, agg_t):
    agg_t[...] = dot(feats[...], adj[...], 1, 1).astype(BF)


def middle_kernel(
    odd, adj, own, paired_in, crossed_in, stale, mark, logits, inner, within, across
):
    blk = within.shape[0]
    is_odd = odd[0] == 1
    up = jnp.where(is_odd, paired_in[...], crossed_in[...])
    down = jnp.where(is_odd, crossed_in[...], paired_in[...])
    size = own.shape[0]
    reach = size + 2 * blk
    agg = dot(adj[:, :blk], up, 1, 0)
    agg += dot(adj[:, blk : blk + size], own[...], 1, 0)
    agg += dot(adj[:, blk + size : reach], down, 1, 0)
    agg += stale[...]
    logits[...] = agg.astype(BF)
    e = jnp.exp(agg - jnp.max(agg, axis=1, keepdims=True))
    grad = (e / jnp.sum(e, axis=1, keepdims=True) - mark[...]).astype(BF)
    spread = dot(adj[:, :reach], grad, 0, 0)
    inner[...] = spread[blk : blk + size]
    rim_up, rim_down = spread[:blk], spread[blk + size :]
    within[...] = jnp.where(is_odd, rim_up, rim_down).astype(BF)
    across[...] = jnp.where(is_odd, rim_down, rim_up).astype(BF)


def backward_kernel(
    scale, odd, core, inner, paired_in, crossed_in, hidden, w_second, slope, agg_t, send, kept, grad_agg, second
):
    blk = paired_in.shape[0]
    size = inner.shape[0]
    hid = slope.shape[1]
    step = min(256, hid)
    half = hid // 2
    is_odd = odd[0] == 1
    mine, other = core[0], 1 - core[0]
    upper = inner[:blk] + jnp.where(is_odd, paired_in[...], crossed_in[...]).astype(F32)
    lower = inner[size - blk :] + jnp.where(is_odd, crossed_in[...], paired_in[...]).astype(F32)
    if size > 2 * blk:
        parts = [upper, inner[blk : size - blk], lower]
    else:
        parts = [upper, lower]
    grad_p2 = jnp.concatenate(parts, axis=0).astype(BF)
    for at in range(0, hid, step):
        cols = slice(at, at + step)
        grad_agg[:, cols] = (dot(grad_p2, w_second[cols, :], 1, 1) * slope[:, cols].astype(F32)).astype(BF)
    second[...] = (dot(hidden[...], grad_p2, 0, 0) * scale).reshape(second.shape)
    rows = second.shape[0] * second.shape[2]
    send[:, half:] = second[:, other].reshape(rows, second.shape[3]).astype(BF)
    kept[...] = second[:, mine].reshape(rows, second.shape[3])
    g = grad_agg[:, pl.ds(pl.multiple_of(other * half, half), half)]
    send[:, :half] = (dot(agg_t[...], g, 1, 0) * scale).astype(BF)


def feature_kernel(scale, core, grad_agg, adj, agg_t, kept, w_first_far, keep, out, w_first, sem):
    fetch = pltpu.make_async_copy(w_first_far, w_first, sem)
    fetch.start()
    width = out.shape[1]
    half = grad_agg.shape[1] // 2
    g = grad_agg[:, pl.ds(pl.multiple_of(core[0] * half, half), half)]
    keep[:, :half] = dot(agg_t[...], g, 1, 0) * scale
    keep[:, half:] = kept[...]
    fetch.wait()
    back = dot(w_first[...], grad_agg[...], 1, 1).astype(BF)
    out[...] = dot(back, adj[:, :width], 1, 0).astype(BF)


def whole_core(kernel, outs, blocks, scratch=(), flops=0, scalars=1, fetched=0):
    return pl.pallas_call(
        kernel,
        out_shape=[jax.ShapeDtypeStruct(*out) for out in outs],
        in_specs=[pl.BlockSpec(memory_space=pltpu.SMEM)] * scalars + [pl.BlockSpec(memory_space=pltpu.VMEM)] * blocks
        + [pl.BlockSpec(memory_space=pl.ANY)] * fetched,
        scratch_shapes=scratch,
        compiler_params=pltpu.CompilerParams(vmem_limit_bytes=16 * 1024 * 1024),
        cost_estimate=pl.CostEstimate(flops=flops, bytes_accessed=4_000_000, transcendentals=0),
    )


def local(feats_t, w_first, w_second, stale_rows, tile_vals, tile_src, tile_count, labels):
    blk = tile_vals.shape[-1]
    hid = w_first.shape[1]
    classes = w_second.shape[1]
    own = labels.shape[0]
    reach = own + 2 * blk
    n_grp, n_dom = lax.axis_size("grp"), lax.axis_size("dom")
    scale = 1.0 / math.sqrt(own * n_grp * n_dom)
    feat_rows = feats_t.shape[0]
    feat_all = feat_rows * n_dom
    half = hid // 2
    core = lax.axis_index("grp") % 2

    (wide,) = whole(widen_kernel, [((n_dom, feat_rows, reach), BF)])(feats_t)
    wide, tile_vals, stale_rows = lax.optimization_barrier((wide, tile_vals, stale_rows))
    feats = lax.all_to_all(wide, "dom", split_axis=0, concat_axis=0, tiled=True).reshape(feat_all, reach)

    adj, adj_stale = whole_core(adjacency_kernel, [((own, reach), BF), ((own, 2 * blk), BF)], 1, scalars=2)(
        tile_src, tile_count, tile_vals
    )
    before = from_previous(stale_rows, "grp")
    after = from_next(stale_rows, "grp")
    stale_first, stale_second = whole(
        stale_kernel,
        [((own, hid), BF), ((own, classes), F32)],
        scratch=[pltpu.VMEM((2 * blk, hid + classes), BF)],
        flops=2 * own * 2 * blk * (hid + classes),
    )(adj_stale, before, after)
    mark = (labels[:, None] == jnp.arange(classes, dtype=jnp.int32)[None, :]).astype(F32)

    odd = ((lax.axis_index("dom") + 1) % 2)[None]
    hidden, slope, proj_second, within, across = whole_core(
        forward_kernel,
        [
            ((own, hid), BF),
            ((own, hid), BF),
            ((own, classes), BF),
            ((blk, classes), BF),
            ((blk, classes), BF),
        ],
        4,
        scratch=[pltpu.VMEM((hid, classes), BF), pltpu.SemaphoreType.DMA],
        fetched=1,
        flops=2 * own * (feat_all * reach + feat_all * hid + hid * classes),
    )(odd, adj, feats, w_first, stale_first, in_hbm(w_second))
    feats, adj_beside, within = lax.optimization_barrier((feats, adj, within))
    (agg_t,) = whole(aggregate_kernel, [((feat_all, own), BF)], flops=2 * own * feat_all * reach)(feats, adj_beside)

    logits, inner, within, across = whole_core(
        middle_kernel,
        [((own, classes), BF), ((own, classes), F32), ((blk, classes), BF), ((blk, classes), BF)],
        6,
        flops=4 * own * reach * classes,
    )(
        odd,
        adj,
        proj_second,
        paired(within, "dom", 1),
        paired(across, "dom", 0),
        stale_second,
        mark,
    )

    width = half + classes
    send, kept, grad_agg = whole_core(
        functools.partial(backward_kernel, scale),
        [((feat_all, width), BF), ((feat_all, classes), F32), ((own, hid), BF)],
        7,
        scratch=[pltpu.VMEM((n_dom, 2, feat_rows, classes), F32)],
        flops=2 * own * (hid * classes * 2 + feat_all * half),
        scalars=2,
    )(odd, core[None], inner, paired(within, "dom", 1), paired(across, "dom", 0), hidden, w_second, slope, agg_t)
    received = swapped(send, "grp")

    keep, grad_wide = whole_core(
        functools.partial(feature_kernel, scale),
        [((feat_all, width), F32), ((feat_all, reach), BF)],
        4,
        scratch=[pltpu.VMEM((feat_all, hid), BF), pltpu.SemaphoreType.DMA],
        fetched=1,
        flops=2 * own * (hid * feat_all + reach * feat_all + feat_all * half),
    )(core[None], grad_agg, adj, agg_t, kept, in_hbm(w_first))
    summed = (keep + received.astype(F32)).astype(BF)
    sent = jnp.concatenate([summed, grad_wide], axis=1)
    got = lax.all_to_all(sent, "dom", split_axis=0, concat_axis=0, tiled=True).reshape(n_dom, feat_rows, -1)

    band = jnp.sum(got[:, :, :width].astype(F32), axis=0).astype(BF)
    copies = jnp.broadcast_to(band[None], (n_grp, feat_rows, width))
    bands = lax.all_to_all(copies, "grp", split_axis=0, concat_axis=0, tiled=True)
    grad_first, grad_second = whole(
        total_kernel, [((feat_rows, hid), F32), ((2 * feat_rows, classes), F32)]
    )(bands)

    wide_back = got[:, :, width:].astype(F32)
    none = jnp.zeros((1, feat_rows, blk), F32)
    first_block = jnp.concatenate([none, wide_back[:-1, :, reach - blk :]], axis=0)
    last_block = jnp.concatenate([wide_back[1:, :, :blk], none], axis=0)
    middle = jnp.zeros((n_dom, feat_rows, own - blk), F32)
    grad_feats = (
        wide_back[:, :, blk : reach - blk]
        + jnp.concatenate([first_block, middle], axis=2)
        + jnp.concatenate([middle, last_block], axis=2)
    )
    grad_feats = grad_feats.astype(BF).transpose(1, 0, 2).reshape(feat_rows, n_dom * own)
    return (logits, grad_feats, grad_first, grad_second)


def solution(mesh):
    return jax.shard_map(
        local,
        mesh=mesh,
        in_specs=(
            P("dom", "grp"),
            P(),
            P(),
            P(("grp", "dom"), None),
            P(("grp", "dom"), None, None, None),
            P(("grp", "dom"), None),
            P(("grp", "dom")),
            P(("grp", "dom")),
        ),
        out_specs=(P(("grp", "dom"), None), P("dom", "grp"), P("dom", None), P("dom", None)),
        check_vma=False,
    )
```

```python
import functools
import math

import jax
import jax.numpy as jnp
from jax import lax
from jax.experimental import pallas as pl
from jax.experimental.pallas import tpu as pltpu
from jax.sharding import PartitionSpec as P

BF = jnp.bfloat16
F32 = jnp.float32


def dot(a, b, ca, cb):
    return lax.dot_general(a, b, (((ca,), (cb,)), ((), ())), preferred_element_type=F32)


def swapped(x, axis):
    count = lax.axis_size(axis)
    return lax.ppermute(x, axis, [(i, i ^ 1) for i in range(count)])


def from_previous(x, axis):
    count = lax.axis_size(axis)
    return lax.ppermute(x, axis, [(i, i + 1) for i in range(count - 1)])


def from_next(x, axis):
    count = lax.axis_size(axis)
    return lax.ppermute(x, axis, [(i + 1, i) for i in range(count - 1)])


def paired(x, axis, first):
    count = lax.axis_size(axis)
    pairs = []
    for i in range(first, count - 1, 2):
        pairs += [(i, i + 1), (i + 1, i)]
    return lax.ppermute(x, axis, pairs)


def in_hbm(x):
    return pltpu.with_memory_space_constraint(x, pltpu.HBM)


def whole(kernel, outs, scratch=(), flops=0):
    return pl.pallas_call(
        kernel,
        out_shape=[jax.ShapeDtypeStruct(*out) for out in outs],
        scratch_shapes=list(scratch),
        compiler_params=pltpu.CompilerParams(vmem_limit_bytes=16 * 1024 * 1024),
        cost_estimate=pl.CostEstimate(flops=flops, bytes_accessed=4_000_000, transcendentals=0),
    )


def widen_kernel(feats, wide):
    parts, rows, reach = wide.shape
    own = feats.shape[1] // parts
    blk = (reach - own) // 2
    none = jnp.zeros((rows, blk), wide.dtype)
    for d in range(parts):
        first, last = d * own - blk, (d + 1) * own + blk
        wide[d, :, blk : blk + own] = feats[:, d * own : (d + 1) * own]
        wide[d, :, :blk] = feats[:, first : first + blk] if d > 0 else none
        wide[d, :, blk + own :] = feats[:, last - blk : last] if d < parts - 1 else none


def adjacency_kernel(src, count, tiles, adj, adj_stale):
    block_rows, slots, blk, _ = tiles.shape
    for r in range(block_rows):
        live = count[r]
        inside = adj.shape[1] // blk
        for t in range(inside + adj_stale.shape[1] // blk):
            block = jnp.zeros((blk, blk), BF)
            for k in range(slots):
                hit = jnp.logical_and(src[r, k] == t, k < live)
                block = jnp.where(hit, tiles[r, k], block)
            out, at = (adj, t) if t < inside else (adj_stale, t - inside)
            out[r * blk : (r + 1) * blk, at * blk : (at + 1) * blk] = block


def total_kernel(bands, first, second):
    cores, half = 2, first.shape[1] // 2
    rows = first.shape[0]
    for c in range(cores):
        total = bands[c].astype(F32)
        for z in range(1, bands.shape[0] // cores):
            total += bands[z * cores + c].astype(F32)
        first[:, c * half : (c + 1) * half] = total[:, :half]
        second[c * rows : (c + 1) * rows, :] = total[:, half:]


def stale_kernel(adj_stale, before, after, first, second, rows):
    count = before.shape[0]
    rows[:count] = before[...]
    rows[count:] = after[...]
    hid = first.shape[1]
    first[...] = dot(adj_stale[...], rows[:, :hid], 1, 0).astype(BF)
    second[...] = dot(adj_stale[...], rows[:, hid:], 1, 0)


def forward_kernel(
    odd, adj, feats, w_first, stale, w_second_far, hidden, slope, proj, within, across, w_second, sem
):
    fetch = pltpu.make_async_copy(w_second_far, w_second, sem)
    fetch.start()
    hid = w_first.shape[1]
    step = min(256, hid)
    agg = dot(adj[...], feats[...], 1, 1).astype(BF)
    for at in range(0, hid, step):
        cols = slice(at, at + step)
        a = dot(agg, w_first[:, cols], 1, 0) + stale[:, cols].astype(F32)
        s = jax.nn.sigmoid(a)
        hidden[:, cols] = (a * s).astype(BF)
        slope[:, cols] = (s * (1.0 + a * (1.0 - s))).astype(BF)
    fetch.wait()
    proj[...] = dot(hidden[...], w_second[...], 1, 0).astype(BF)
    blk = within.shape[0]
    top, bottom = proj[:blk], proj[proj.shape[0] - blk :]
    is_odd = odd[0] == 1
    within[...] = jnp.where(is_odd, top, bottom)
    across[...] = jnp.where(is_odd, bottom, top)


def turn_kernel(adj, adj_t):
    adj_t[...] = adj[...].T


def aggregate_kernel(feats, adj, agg_t):
    agg_t[...] = dot(feats[...], adj[...], 1, 1).astype(BF)


def middle_kernel(
    odd, adj, adj_t, own, paired_in, crossed_in, stale, mark, logits, inner, within, across
):
    blk = within.shape[0]
    is_odd = odd[0] == 1
    up = jnp.where(is_odd, paired_in[...], crossed_in[...])
    down = jnp.where(is_odd, crossed_in[...], paired_in[...])
    size = own.shape[0]
    reach = size + 2 * blk
    agg = dot(adj[:, :blk], up, 1, 0)
    agg += dot(adj[:, blk : blk + size], own[...], 1, 0)
    agg += dot(adj[:, blk + size : reach], down, 1, 0)
    agg += stale[...]
    logits[...] = agg.astype(BF)
    e = jnp.exp(agg - jnp.max(agg, axis=1, keepdims=True))
    grad = (e / jnp.sum(e, axis=1, keepdims=True) - mark[...]).astype(BF)
    spread = dot(adj_t[...], grad, 1, 0)
    inner[...] = spread[blk : blk + size]
    rim_up, rim_down = spread[:blk], spread[blk + size :]
    within[...] = jnp.where(is_odd, rim_up, rim_down).astype(BF)
    across[...] = jnp.where(is_odd, rim_down, rim_up).astype(BF)


def backward_kernel(
    scale, odd, core, inner, paired_in, crossed_in, hidden, w_second, slope, agg_t, send, kept, grad_agg, second
):
    blk = paired_in.shape[0]
    size = inner.shape[0]
    hid = slope.shape[1]
    step = min(256, hid)
    half = hid // 2
    is_odd = odd[0] == 1
    mine, other = core[0], 1 - core[0]
    upper = inner[:blk] + jnp.where(is_odd, paired_in[...], crossed_in[...]).astype(F32)
    lower = inner[size - blk :] + jnp.where(is_odd, crossed_in[...], paired_in[...]).astype(F32)
    if size > 2 * blk:
        parts = [upper, inner[blk : size - blk], lower]
    else:
        parts = [upper, lower]
    grad_p2 = jnp.concatenate(parts, axis=0).astype(BF)
    for at in range(0, hid, step):
        cols = slice(at, at + step)
        grad_agg[:, cols] = (dot(grad_p2, w_second[cols, :], 1, 1) * slope[:, cols].astype(F32)).astype(BF)
    second[...] = (dot(hidden[...], grad_p2, 0, 0) * scale).reshape(second.shape)
    rows = second.shape[0] * second.shape[2]
    send[:, half:] = second[:, other].reshape(rows, second.shape[3]).astype(BF)
    kept[...] = second[:, mine].reshape(rows, second.shape[3])
    g = grad_agg[:, pl.ds(pl.multiple_of(other * half, half), half)]
    send[:, :half] = (dot(agg_t[...], g, 1, 0) * scale).astype(BF)


def feature_kernel(scale, core, grad_agg, adj, agg_t, kept, w_first_far, keep, out, w_first, sem):
    fetch = pltpu.make_async_copy(w_first_far, w_first, sem)
    fetch.start()
    width = out.shape[1]
    half = grad_agg.shape[1] // 2
    g = grad_agg[:, pl.ds(pl.multiple_of(core[0] * half, half), half)]
    keep[:, :half] = dot(agg_t[...], g, 1, 0) * scale
    keep[:, half:] = kept[...]
    fetch.wait()
    back = dot(w_first[...], grad_agg[...], 1, 1).astype(BF)
    out[...] = dot(back, adj[:, :width], 1, 0).astype(BF)


def whole_core(kernel, outs, blocks, scratch=(), flops=0, scalars=1, fetched=0):
    return pl.pallas_call(
        kernel,
        out_shape=[jax.ShapeDtypeStruct(*out) for out in outs],
        in_specs=[pl.BlockSpec(memory_space=pltpu.SMEM)] * scalars + [pl.BlockSpec(memory_space=pltpu.VMEM)] * blocks
        + [pl.BlockSpec(memory_space=pl.ANY)] * fetched,
        scratch_shapes=scratch,
        compiler_params=pltpu.CompilerParams(vmem_limit_bytes=16 * 1024 * 1024),
        cost_estimate=pl.CostEstimate(flops=flops, bytes_accessed=4_000_000, transcendentals=0),
    )


def local(feats_t, w_first, w_second, stale_rows, tile_vals, tile_src, tile_count, labels):
    blk = tile_vals.shape[-1]
    hid = w_first.shape[1]
    classes = w_second.shape[1]
    own = labels.shape[0]
    reach = own + 2 * blk
    n_grp, n_dom = lax.axis_size("grp"), lax.axis_size("dom")
    scale = 1.0 / math.sqrt(own * n_grp * n_dom)
    feat_rows = feats_t.shape[0]
    feat_all = feat_rows * n_dom
    half = hid // 2
    core = lax.axis_index("grp") % 2

    (wide,) = whole(widen_kernel, [((n_dom, feat_rows, reach), BF)])(feats_t)
    wide, tile_vals, stale_rows = lax.optimization_barrier((wide, tile_vals, stale_rows))
    feats = lax.all_to_all(wide, "dom", split_axis=0, concat_axis=0, tiled=True).reshape(feat_all, reach)

    adj, adj_stale = whole_core(adjacency_kernel, [((own, reach), BF), ((own, 2 * blk), BF)], 1, scalars=2)(
        tile_src, tile_count, tile_vals
    )
    before = from_previous(stale_rows, "grp")
    after = from_next(stale_rows, "grp")
    stale_first, stale_second = whole(
        stale_kernel,
        [((own, hid), BF), ((own, classes), F32)],
        scratch=[pltpu.VMEM((2 * blk, hid + classes), BF)],
        flops=2 * own * 2 * blk * (hid + classes),
    )(adj_stale, before, after)
    mark = (labels[:, None] == jnp.arange(classes, dtype=jnp.int32)[None, :]).astype(F32)

    odd = ((lax.axis_index("dom") + 1) % 2)[None]
    hidden, slope, proj_second, within, across = whole_core(
        forward_kernel,
        [
            ((own, hid), BF),
            ((own, hid), BF),
            ((own, classes), BF),
            ((blk, classes), BF),
            ((blk, classes), BF),
        ],
        4,
        scratch=[pltpu.VMEM((hid, classes), BF), pltpu.SemaphoreType.DMA],
        fetched=1,
        flops=2 * own * (feat_all * reach + feat_all * hid + hid * classes),
    )(odd, adj, feats, w_first, stale_first, in_hbm(w_second))
    feats, adj_beside, within = lax.optimization_barrier((feats, adj, within))
    (agg_t,) = whole(aggregate_kernel, [((feat_all, own), BF)], flops=2 * own * feat_all * reach)(feats, adj_beside)

    (adj_t,) = whole(turn_kernel, [((reach, own), BF)])(adj_beside)
    logits, inner, within, across = whole_core(
        middle_kernel,
        [((own, classes), BF), ((own, classes), F32), ((blk, classes), BF), ((blk, classes), BF)],
        7,
        flops=4 * own * reach * classes,
    )(
        odd,
        adj,
        adj_t,
        proj_second,
        paired(within, "dom", 1),
        paired(across, "dom", 0),
        stale_second,
        mark,
    )

    width = half + classes
    send, kept, grad_agg = whole_core(
        functools.partial(backward_kernel, scale),
        [((feat_all, width), BF), ((feat_all, classes), F32), ((own, hid), BF)],
        7,
        scratch=[pltpu.VMEM((n_dom, 2, feat_rows, classes), F32)],
        flops=2 * own * (hid * classes * 2 + feat_all * half),
        scalars=2,
    )(odd, core[None], inner, paired(within, "dom", 1), paired(across, "dom", 0), hidden, w_second, slope, agg_t)
    received = swapped(send, "grp")

    keep, grad_wide = whole_core(
        functools.partial(feature_kernel, scale),
        [((feat_all, width), F32), ((feat_all, reach), BF)],
        4,
        scratch=[pltpu.VMEM((feat_all, hid), BF), pltpu.SemaphoreType.DMA],
        fetched=1,
        flops=2 * own * (hid * feat_all + reach * feat_all + feat_all * half),
    )(core[None], grad_agg, adj, agg_t, kept, in_hbm(w_first))
    summed = (keep + received.astype(F32)).astype(BF)
    sent = jnp.concatenate([summed, grad_wide], axis=1)
    got = lax.all_to_all(sent, "dom", split_axis=0, concat_axis=0, tiled=True).reshape(n_dom, feat_rows, -1)

    band = jnp.sum(got[:, :, :width].astype(F32), axis=0).astype(BF)
    copies = jnp.broadcast_to(band[None], (n_grp, feat_rows, width))
    bands = lax.all_to_all(copies, "grp", split_axis=0, concat_axis=0, tiled=True)
    grad_first, grad_second = whole(
        total_kernel, [((feat_rows, hid), F32), ((2 * feat_rows, classes), F32)]
    )(bands)

    wide_back = got[:, :, width:].astype(F32)
    none = jnp.zeros((1, feat_rows, blk), F32)
    first_block = jnp.concatenate([none, wide_back[:-1, :, reach - blk :]], axis=0)
    last_block = jnp.concatenate([wide_back[1:, :, :blk], none], axis=0)
    middle = jnp.zeros((n_dom, feat_rows, own - blk), F32)
    grad_feats = (
        wide_back[:, :, blk : reach - blk]
        + jnp.concatenate([first_block, middle], axis=2)
        + jnp.concatenate([middle, last_block], axis=2)
    )
    grad_feats = grad_feats.astype(BF).transpose(1, 0, 2).reshape(feat_rows, n_dom * own)
    return (logits, grad_feats, grad_first, grad_second)


def solution(mesh):
    return jax.shard_map(
        local,
        mesh=mesh,
        in_specs=(
            P("dom", "grp"),
            P(),
            P(),
            P(("grp", "dom"), None),
            P(("grp", "dom"), None, None, None),
            P(("grp", "dom"), None),
            P(("grp", "dom")),
            P(("grp", "dom")),
        ),
        out_specs=(P(("grp", "dom"), None), P("dom", "grp"), P("dom", None), P("dom", None)),
        check_vma=False,
    )
```
